32 devices in a mesh: groups: 2 (over x), inst: 8 (over z, y), tp: 2 (over core).
Axes of the slice: x: 2, y: 2, z: 4, core: 2. Of those that a mesh axis runs over, the one named last changes fastest.
Arguments:
- request_dest: int32 [16, 8], P(('groups', 'inst')), parts along dimension 0, may hold values from 0 to 7, as said below
- request_slot: int32 [16, 8], P(('groups', 'inst')), parts along dimension 0, may hold values from 0 to 7, as said below
- page_len: int32 [16, 8], P(('groups', 'inst')), parts along dimension 0, may hold values from 1 to 32
- page_rows: bfloat16 [16, 8, 32, 2, 8, 128], P(('groups', 'inst'), None, None, None, 'tp'), parts along dimension 0, may hold values from -6 to 6
- kv_cache: bfloat16 [16, 1024, 2, 8, 128], P(('groups', 'inst'), None, None, 'tp'), parts along dimension 0, may hold values from -6 to 6
- decode_cache: bfloat16 [16, 64, 2, 8, 128], P(('groups', 'inst'), None, None, 'tp'), parts along dimension 0, may hold values from -6 to 6
- prefix_len: int32 [16], P(('groups', 'inst')), parts along dimension 0, may hold values from 1 to 1024
- cached_len: int32 [16, 8], P(('groups', 'inst')), parts along dimension 0, may hold values from 0 to 8
- queries: bfloat16 [16, 272, 64, 128], P(('groups', 'inst'), None, 'tp'), parts along dimension 0
- fresh_kv: bfloat16 [16, 272, 2, 8, 128], P(('groups', 'inst'), None, None, 'tp'), parts along dimension 0, may hold values from -6 to 6
Outputs:
- attention: bfloat16 [16, 272, 64, 128], P(('groups', 'inst'), None, 'tp'), parts along dimension 0
The draws below stay inside these ranges and needn't reach their ends.
There are 2 independent parts, one for each index of `groups`. The reference program is written for one: setup_inputs(seed, part) draws one part's arguments, and reference() takes and returns one part's arrays. A program takes and returns all parts, laid end to end along the dimension named above; each array names one. Nothing has to cross between parts.
Inputs may be any that keep to these rules, and one draw needn't show every extreme that they name: `request_dest`: each instance's requests name 4 distinct instances, 2 requests each; every instance is named by exactly 8 requests in all. `request_slot`: the requests that reach one instance have distinct slots, so every slot of every instance is taken.
All inputs are finite; a program needn't handle non-finite values.
Results may differ from the reference program's by a relative error of at most 0.0045.
Values may be sent and summed in bfloat16 or wider, within the bound.
No kernel may reach another device: no remote copies, remote signals or barrier semaphores. Data moves between devices by JAX's collectives and lax.ppermute only.
A program may use at most 192 MiB of HBM per device.

```python
import math
import jax
import jax.numpy as jnp
from jax import lax

HQ = 64
KVH = 8
HD = 128
PAIR = 2
TAIL = 256
PAGE = 32
CTX = 1024
CACHE = 8
REQ = 8
SLOTS = 8
N_INST = 8


def serving_plan(key):
    first = jax.random.permutation(jax.random.fold_in(key, 101), N_INST).astype(jnp.int32)
    second = jax.random.permutation(jax.random.fold_in(key, 102), N_INST).astype(jnp.int32)
    offsets = jax.random.permutation(jax.random.fold_in(key, 103), N_INST).astype(jnp.int32)[:N_INST // 2]
    row_keys = jax.random.split(jax.random.fold_in(key, 104), N_INST)
    spot_order = jax.vmap(lambda sub_key: jax.random.permutation(sub_key, REQ))(row_keys).astype(jnp.int32)
    round_of = spot_order // PAIR
    dest_drawn = second[(first[:, None] + offsets[round_of]) % N_INST]
    arrival = round_of * PAIR + spot_order % PAIR
    slot_keys = jax.random.split(jax.random.fold_in(key, 105), N_INST)
    tables = jax.vmap(lambda sub_key: jax.random.permutation(sub_key, SLOTS))(slot_keys).astype(jnp.int32)
    slot_drawn = tables[dest_drawn, arrival]
    return (dest_drawn, slot_drawn)


def draw_request_dest(key, part):
    return serving_plan(key)[0]


def draw_request_slot(key, part):
    return serving_plan(key)[1]


def draw_page_len(key, part):
    key = jax.random.fold_in(key, 7)
    drawn = jax.random.randint(key, (N_INST, REQ), 1, PAGE + 1, dtype=jnp.int32)
    return drawn.at[0, 0].set(PAGE)


def draw_prefix_len(key, part):
    key = jax.random.fold_in(key, 8)
    base = jax.random.randint(jax.random.fold_in(key, 1), (N_INST,), 1, CTX + 1, dtype=jnp.int32)
    shifts = jax.random.randint(jax.random.fold_in(key, 2), (N_INST,), 0, 4, dtype=jnp.int32)
    drawn = jnp.maximum(jnp.right_shift(base, shifts), 1)
    return drawn.at[0].set(CTX)


def draw_cached_len(key, part):
    key = jax.random.fold_in(key, 9)
    drawn = jax.random.randint(key, (N_INST, SLOTS), 0, CACHE + 1, dtype=jnp.int32)
    return drawn.at[0, 0].set(CACHE)


def draw_queries(key, part):
    key = jax.random.fold_in(key, 10)
    values = jax.random.normal(key, (N_INST, TAIL + 2 * SLOTS, HQ, HD), jnp.float32)
    return values.astype(jnp.bfloat16)


def levels(stream_key, shape, shards, smallest, high):
    factor_of = 1.0
    for axis_at, shards_of in shards:
        draws = jax.random.uniform(jax.random.fold_in(jax.random.fold_in(stream_key, 6), axis_at), (shards_of,), jnp.float32, smallest / len(shards), high / len(shards))
        factor_of = factor_of * jnp.repeat(jnp.exp(draws), shape[axis_at] // shards_of).reshape((-1,) + (1,) * (len(shape) - 1 - axis_at))
    return factor_of


def normal_values(stream_key, extent, deviation, reach, pieces=(), held_as=jnp.bfloat16):
    result = jax.random.normal(stream_key, extent, jnp.float32) * deviation
    if len(pieces) > 0:
        result = levels(stream_key, extent, pieces, -0.22, 0.18) * result
    return jnp.clip(result, min=-reach, max=reach).astype(held_as)


def setup_inputs(seed: int = 0, part: int = 0) -> dict:
    seeds = jax.random.split(jax.random.key(seed), 11)
    part_splits = jax.random.split(jax.random.fold_in(seeds[10], part), 11)
    return {
        "request_dest": draw_request_dest(jax.random.fold_in(jax.random.fold_in(seeds[10], part), 71), part),
        "request_slot": draw_request_slot(jax.random.fold_in(jax.random.fold_in(seeds[10], part), 71), part),
        "page_len": draw_page_len(jax.random.fold_in(jax.random.fold_in(seeds[10], part), 71), part),
        "page_rows": normal_values(part_splits[3], (N_INST, REQ, PAGE, 2, KVH, HD), 1.0, 6.0, ((0, 8), (4, 2))),
        "kv_cache": normal_values(part_splits[4], (N_INST, CTX, 2, KVH, HD), 1.0, 6.0, ((0, 8), (3, 2))),
        "decode_cache": normal_values(part_splits[5], (N_INST, SLOTS * CACHE, 2, KVH, HD), 1.0, 6.0, ((0, 8), (3, 2))),
        "prefix_len": draw_prefix_len(jax.random.fold_in(jax.random.fold_in(seeds[10], part), 71), part),
        "cached_len": draw_cached_len(jax.random.fold_in(jax.random.fold_in(seeds[10], part), 71), part),
        "queries": draw_queries(jax.random.fold_in(jax.random.fold_in(seeds[10], part), 71), part),
        "fresh_kv": normal_values(part_splits[9], (N_INST, TAIL + 2 * SLOTS, 2, KVH, HD), 1.0, 6.0, ((0, 8), (3, 2))),
    }


NEG = -1e+30

def soft_attend(scores, allowed, values, einsum_form):
    masked = jnp.where(allowed, scores, NEG)
    peak_score = lax.optimization_barrier(jnp.max(masked, axis=-1, keepdims=True))
    weights = jnp.where(allowed, jnp.exp(masked - peak_score), 0.0)
    weight_sum = lax.optimization_barrier(jnp.sum(weights, axis=-1))
    rounded = lax.optimization_barrier(weights.astype(jnp.bfloat16)).astype(jnp.float32)
    summed = jnp.einsum(einsum_form, rounded, values.astype(jnp.float32))
    return summed / weight_sum[..., None]

def slot_mask(cached, page_count, cache_depth, page_depth):
    slot_count = cached.shape[0]
    own_ok = jnp.broadcast_to(jnp.arange(cache_depth, dtype=jnp.int32)[None, None, :] < cached[None, :, None], (2, slot_count, cache_depth))
    page_ok = jnp.broadcast_to(jnp.arange(page_depth, dtype=jnp.int32)[None, None, :] < page_count[None, :, None], (2, slot_count, page_depth))
    steps_ok = jnp.broadcast_to(jnp.arange(2, dtype=jnp.int32)[None, None, :] <= jnp.arange(2, dtype=jnp.int32)[:, None, None], (2, slot_count, 2))
    return jnp.concatenate([own_ok, page_ok, steps_ok], -1)

def prefill_rows(query_rows, cache_rows, fresh_rows, prefix):
    tail_count, head_count, head_width = query_rows.shape
    kv_count = cache_rows.shape[2]
    grouped = query_rows.astype(jnp.float32).reshape(tail_count, kv_count, head_count // kv_count, head_width)
    key_value = jnp.concatenate([cache_rows, fresh_rows], 0).astype(jnp.float32)
    scores = jnp.einsum('tkgd,jkd->kgtj', grouped, key_value[:, 0]) / math.sqrt(head_width)
    cache_depth = cache_rows.shape[0]
    column_ids = jnp.arange(cache_depth + tail_count, dtype=jnp.int32)[None, :]
    row_ids = jnp.arange(tail_count, dtype=jnp.int32)[:, None]
    allowed = jnp.where(column_ids < cache_depth, column_ids < prefix, column_ids - cache_depth <= row_ids)
    mixed = soft_attend(scores, allowed[None, None], key_value[:, 1], 'kgtj,jkd->kgtd')
    return jnp.transpose(mixed, (2, 0, 1, 3)).reshape(tail_count, head_count, head_width)

def decode_rows(query_rows, cache_rows, fresh_rows, cached, page_rows, page_count):
    row_count, head_count, head_width = query_rows.shape
    slot_count = cached.shape[0]
    kv_count = cache_rows.shape[2]
    cache_depth = cache_rows.shape[0] // slot_count
    page_depth = page_rows.shape[1]
    grouped = query_rows.astype(jnp.float32).reshape(2, slot_count, kv_count, head_count // kv_count, head_width)
    own_rows = cache_rows.reshape(slot_count, cache_depth, 2, kv_count, head_width)
    new_rows = jnp.swapaxes(fresh_rows.reshape(2, slot_count, 2, kv_count, head_width), 0, 1)
    key_value = jnp.concatenate([own_rows, page_rows, new_rows], 1).astype(jnp.float32)
    scores = jnp.einsum('eskgd,sjkd->eskgj', grouped, key_value[:, :, 0]) / math.sqrt(head_width)
    allowed = slot_mask(cached, page_count, cache_depth, page_depth)
    mixed = soft_attend(scores, allowed[:, :, None, None, :], key_value[:, :, 1], 'eskgj,sjkd->eskgd')
    return mixed.reshape(row_count, head_count, head_width)

def reference(request_dest, request_slot, page_len, page_rows, kv_cache, decode_cache, prefix_len, cached_len, queries, fresh_kv):
    members, request_count = request_dest.shape
    slot_count = cached_len.shape[1]
    tail_count = queries.shape[1] - 2 * slot_count
    flat_ids = jnp.arange(members * request_count, dtype=jnp.int32).reshape(members, request_count)
    table = jnp.full((members, slot_count), -1, jnp.int32).at[request_dest, request_slot].set(flat_ids, mode='drop')
    lengths = jnp.zeros((members, slot_count), jnp.int32).at[request_dest, request_slot].set(page_len, mode='drop')
    flat_pages = page_rows.reshape((members * request_count,) + page_rows.shape[2:])

    def one_instance(position):
        tail_out = prefill_rows(queries[position, :tail_count], kv_cache[position], fresh_kv[position, :tail_count], prefix_len[position])
        picked = flat_pages[jnp.maximum(table[position], 0)]
        step_out = decode_rows(queries[position, tail_count:], decode_cache[position], fresh_kv[position, tail_count:], cached_len[position], picked, lengths[position])
        return jnp.concatenate([tail_out, step_out], 0).astype(jnp.bfloat16)
    return lax.map(one_instance, jnp.arange(members, dtype=jnp.int32))
```

```python
import functools
import math

import jax
import jax.numpy as jnp
from jax import lax
from jax.experimental import pallas as pl
from jax.experimental.pallas import tpu as pltpu
from jax.sharding import PartitionSpec as P

PAIR = 2
NEG = -1e30
F32 = jnp.float32
BF16 = jnp.bfloat16
META = 16
MIB = 1 << 20


def nt_dot(a, b):
    return lax.dot_general(a, b, (((1,), (1,)), ((), ())), preferred_element_type=F32)


def nn_dot(a, b):
    return jnp.dot(a, b, preferred_element_type=F32)


def unmix(kinds, rows):
    keys = rows // kinds
    i = lax.broadcasted_iota(jnp.int32, (rows, rows), 0)
    j = lax.broadcasted_iota(jnp.int32, (rows, rows), 1)
    return jnp.where(j == (i % keys) * kinds + i // keys, 1.0, 0.0).astype(BF16)


def scaled_queries(q, scale):
    q = q * scale
    high = q.astype(BF16)
    low = (q - high.astype(F32)).astype(BF16)
    return jnp.concatenate([high, low], axis=1)


def twice(k):
    return jnp.concatenate([k, k], axis=1)


def with_ones(v):
    return jnp.concatenate([v, jnp.ones_like(v)], axis=1)


def pack_kernel(split, me_ref, dest_ref, slot_ref, len_ref, pages_ref, *refs):
    if split:
        members = len(refs) - 5
        buffers = refs[:members]
    else:
        members = refs[0].shape[0]
        buffers = [refs[0].at[k] for k in range(members)]
    zeros, meta, page_sem, meta_sem, zero_sem = refs[-5:]
    requests = pages_ref.shape[0]
    page_rows = pages_ref.shape[1]
    depth = 32
    me = me_ref[0]
    peer, place = [], []
    for r in range(requests):
        target = dest_ref[0, r]
        earlier = jnp.int32(0)
        for q in range(r):
            earlier = earlier + jnp.where(dest_ref[0, q] == target, 1, 0)
        peer.append(target ^ me if split else target)
        place.append(earlier)
    for r in range(requests):
        begin = pl.multiple_of(place[r] * page_rows, page_rows)
        if split:
            for k in range(members):

                @pl.when(peer[r] == k)
                def _():
                    pltpu.make_async_copy(
                        pages_ref.at[r], buffers[k].at[pl.ds(begin, page_rows), :], page_sem
                    ).start()

        else:
            pltpu.make_async_copy(
                pages_ref.at[r], refs[0].at[peer[r], pl.ds(begin, page_rows), :], page_sem
            ).start()
    zeros[...] = jnp.zeros_like(zeros)
    lane = lax.broadcasted_iota(jnp.int32, (META, 128), 1)
    half = (lane // depth) % PAIR
    used = []
    for k in range(members):
        code = jnp.full((META, 128), -1.0, F32)
        count = jnp.int32(0)
        for r in range(requests):
            mine = peer[r] == k
            count = count + jnp.where(mine, 1, 0)
            live = jnp.where(mine, len_ref[0, r], 0)
            here = (half == place[r]) & (lane % depth < live)
            code = jnp.where(here, slot_ref[0, r].astype(F32), code)
        meta[k] = code.astype(BF16)
        used.append(count)
        pltpu.make_async_copy(
            meta.at[k], buffers[k].at[pl.ds(PAIR * page_rows, META), :], meta_sem
        ).start()

        @pl.when(count == 0)
        def _():
            pltpu.make_async_copy(
                zeros, buffers[k].at[pl.ds(0, PAIR * page_rows), :], zero_sem
            ).start()

    for r in range(requests):
        pltpu.make_async_copy(
            pages_ref.at[0], buffers[0].at[pl.ds(0, page_rows), :], page_sem
        ).wait()
    for k in range(members):
        pltpu.make_async_copy(
            meta.at[k], buffers[k].at[pl.ds(PAIR * page_rows, META), :], meta_sem
        ).wait()

        @pl.when(used[k] == 0)
        def _():
            pltpu.make_async_copy(
                zeros, buffers[k].at[pl.ds(0, PAIR * page_rows), :], zero_sem
            ).wait()


def pack(split, members, me, dest, slot, length, pages):
    rows = PAIR * pages.shape[1] + META
    if split:
        out_shape = [jax.ShapeDtypeStruct((rows, 128), BF16)] * members
    else:
        out_shape = [jax.ShapeDtypeStruct((members, rows, 128), BF16)]
    smem = pl.BlockSpec(memory_space=pltpu.SMEM)
    hbm = pl.BlockSpec(memory_space=pl.ANY)
    return pl.pallas_call(
        functools.partial(pack_kernel, split),
        out_shape=out_shape,
        in_specs=[smem] * 4 + [hbm],
        out_specs=[hbm] * len(out_shape),
        scratch_shapes=[
            pltpu.VMEM((PAIR * pages.shape[1], 128), BF16),
            pltpu.VMEM((members, META, 128), BF16),
            pltpu.SemaphoreType.DMA,
            pltpu.SemaphoreType.DMA,
            pltpu.SemaphoreType.DMA,
        ],
        name="pack_pages",
    )(me, dest, slot, length, pages)


def tail_kernel(scale, prefix_ref, q_ref, cache_ref, fresh_ref, o_ref, keys, values, mixed):
    block, heads, width = q_ref.shape[1:]
    kv_heads = keys.shape[0]
    group = heads // kv_heads
    kinds = 2 * kv_heads
    context = cache_ref.shape[0] // kinds
    total = keys.shape[1]
    step = pl.program_id(0)

    @pl.when(step == 0)
    def _():
        order = unmix(kinds, 256)
        depth = 256 // kinds
        for at in range(0, total, 2 * depth):
            source, base = (cache_ref, at) if at < context else (fresh_ref, at - context)
            first = source[base * kinds : base * kinds + 256, :]
            second = source[base * kinds + 256 : base * kinds + 512, :]
            sorted_rows = nn_dot(order, jnp.concatenate([first, second], axis=1)).astype(BF16)
            for half in range(2):
                spot = slice(at + half * depth, at + (half + 1) * depth)
                for h in range(kv_heads):
                    rows = sorted_rows[:, half * width : (half + 1) * width]
                    keys[h, spot, :] = rows[h * depth : (h + 1) * depth]
                    values[h, spot, :] = rows[(kv_heads + h) * depth : (kv_heads + h + 1) * depth]

    rows = block * group
    prefix = prefix_ref[0]
    column = lax.broadcasted_iota(jnp.int32, (rows, total), 1)
    row = step * block + lax.broadcasted_iota(jnp.int32, (rows, total), 0) // group
    limit = jnp.where(column < context, prefix, row + context + 1)
    allowed = column < limit
    queries = q_ref[0].astype(F32).reshape(block, kv_heads, group, width)
    for h in range(kv_heads):
        q = scaled_queries(queries[:, h].reshape(rows, width), scale)
        scores = jnp.where(allowed, nt_dot(q, twice(keys[h])), NEG)
        peak = jnp.max(scores, axis=1, keepdims=True)
        weights = jnp.exp2(scores - peak).astype(BF16)
        summed = nn_dot(weights, with_ones(values[h]))
        out = summed[:, :width] / summed[:, width:]
        mixed[:, h] = out.reshape(block, group, width)
    o_ref[0] = mixed[...].reshape(block, heads, width).astype(BF16)


def tail_attention(prefix, queries, cache, fresh, tail_count, kv_heads):
    _, row_count, heads, width = queries.shape
    block = 32
    context = cache.shape[0] // (2 * kv_heads)
    total = context + tail_count
    scale = math.log2(math.e) / math.sqrt(width)
    spec = pl.BlockSpec((1, block, heads, width), lambda i: (0, i, 0, 0))
    whole = lambda a: pl.BlockSpec(a.shape, lambda i: (0, 0))
    return pl.pallas_call(
        functools.partial(tail_kernel, scale),
        grid=(tail_count // block,),
        out_shape=jax.ShapeDtypeStruct(queries.shape, BF16),
        in_specs=[pl.BlockSpec(memory_space=pltpu.SMEM), spec, whole(cache), whole(fresh)],
        out_specs=spec,
        scratch_shapes=[
            pltpu.VMEM((kv_heads, total, width), BF16),
            pltpu.VMEM((kv_heads, total, width), BF16),
            pltpu.VMEM((block, kv_heads, heads // kv_heads, width), F32),
        ],
        compiler_params=pltpu.CompilerParams(vmem_limit_bytes=40 * MIB),
        cost_estimate=pl.CostEstimate(
            flops=4 * tail_count * heads * total * width * 4,
            bytes_accessed=8 * MIB,
            transcendentals=tail_count * heads * total,
        ),
        name="tail_attention",
    )(prefix, queries, cache, fresh)


def row_place(rows, columns, group, slots):
    row = lax.broadcasted_iota(jnp.int32, (rows, columns), 0) // group
    return row % slots, row // slots


def local_kernel(scale, slots, code_ref, q_ref, own_ref, new_ref, m_ref, l_ref, a_ref, keys, values):
    count, heads, width = q_ref.shape
    kv_heads = keys.shape[0]
    group = heads // kv_heads
    kinds = 2 * kv_heads
    for source, base in ((own_ref, 0), (new_ref, own_ref.shape[0] // kinds)):
        chunk = min(256, source.shape[0])
        order = unmix(kinds, chunk)
        depth = chunk // kinds
        for at in range(source.shape[0] // chunk):
            sorted_rows = nn_dot(order, source[at * chunk : (at + 1) * chunk, :]).astype(BF16)
            spot = slice(base + at * depth, base + (at + 1) * depth)
            for h in range(kv_heads):
                keys[h, spot, :] = sorted_rows[h * depth : (h + 1) * depth]
                values[h, spot, :] = sorted_rows[(kv_heads + h) * depth : (kv_heads + h + 1) * depth]
    rows, total = count * group, keys.shape[1]
    slot, made = row_place(rows, total, group, slots)
    code = code_ref[...]
    allowed = (code == slot) | ((code >= slots) & (code - slots == slot)) | (
        (made >= 1) & (code - 2 * slots == slot)
    )
    queries = q_ref[...].astype(F32).reshape(count, kv_heads, group, width)
    for h in range(kv_heads):
        q = scaled_queries(queries[:, h].reshape(rows, width), scale)
        scores = jnp.where(allowed, nt_dot(q, twice(keys[h])), NEG)
        peak = jnp.max(scores, axis=1, keepdims=True)
        weights = jnp.exp2(scores - peak).astype(BF16)
        summed = nn_dot(weights, with_ones(values[h]))
        m_ref[h] = jnp.broadcast_to(peak, (rows, width))
        l_ref[h] = summed[:, width:]
        a_ref[h] = summed[:, :width]


def local_state(codes, queries, own, new, slots, kv_heads):
    count, heads, width = queries.shape
    rows = count * heads // kv_heads
    total = (own.shape[0] + new.shape[0]) // (2 * kv_heads)
    scale = math.log2(math.e) / math.sqrt(width)
    state = jax.ShapeDtypeStruct((kv_heads, rows, width), F32)
    return pl.pallas_call(
        functools.partial(local_kernel, scale, slots),
        out_shape=[state] * 3,
        scratch_shapes=[
            pltpu.VMEM((kv_heads, total, width), BF16),
            pltpu.VMEM((kv_heads, total, width), BF16),
        ],
        compiler_params=pltpu.CompilerParams(vmem_limit_bytes=40 * MIB),
        cost_estimate=pl.CostEstimate(
            flops=8 * rows * kv_heads * total * width,
            bytes_accessed=3 * MIB,
            transcendentals=rows * kv_heads * total,
        ),
        name="decode_local",
    )(codes, queries, own, new)


def page_kernel(scale, slots, split, q_ref, m_ref, l_ref, a_ref, out_in, *refs):
    out_ref, keys, values, mixed, staged, sem = refs[-6:]
    arrived = refs[:-6]
    count, heads, width = q_ref.shape
    kv_heads = keys.shape[0]
    group = heads // kv_heads
    kinds = 2 * kv_heads
    order = unmix(kinds, 256)
    depth = 256 // kinds
    if split:
        piece = lambda k, a, b: arrived[k][a:b, :]
        members = len(arrived)
    else:
        piece = lambda k, a, b: arrived[0][k, a:b, :]
        members = arrived[0].shape[0]
    rows = count * group
    per = 8
    queries = q_ref[...].astype(F32).reshape(count, kv_heads, group, width)
    scaled = [scaled_queries(queries[:, h].reshape(rows, width), scale) for h in range(kv_heads)]
    state = [(m_ref[h], l_ref[h], a_ref[h]) for h in range(kv_heads)]
    lane = lax.broadcasted_iota(jnp.int32, (1, 128), 1)
    for begin in range(0, members, per):
        codes = []
        for k in range(per):
            both = jnp.concatenate(
                [piece(begin + k, 0, 256), piece(begin + k, 256, 512)], axis=1
            )
            sorted_rows = nn_dot(order, both).astype(BF16)
            for half in range(PAIR):
                at = (PAIR * k + half) * depth
                part = sorted_rows[:, half * width : (half + 1) * width]
                for h in range(kv_heads):
                    keys[h, at : at + depth, :] = part[h * depth : (h + 1) * depth]
                    values[h, at : at + depth, :] = part[
                        (kv_heads + h) * depth : (kv_heads + h + 1) * depth
                    ]
            codes.append(piece(begin + k, 512, 512 + META).astype(F32)[0:1, :])
        code = jnp.concatenate(
            [jnp.where(lane < 64, codes[k], codes[k + 1]) for k in range(0, per, 2)], axis=1
        )
        slot, _ = row_place(rows, code.shape[1], group, slots)
        allowed = code == slot.astype(F32)
        for h in range(kv_heads):
            old_peak, old_sum, old = state[h]
            scores = jnp.where(allowed, nt_dot(scaled[h], twice(keys[h])), NEG)
            peak = jnp.maximum(old_peak, jnp.max(scores, axis=1, keepdims=True))
            weights = jnp.exp2(scores - peak[:, 0:1]).astype(BF16)
            summed = nn_dot(weights, with_ones(values[h]))
            shrink = jnp.exp2(old_peak - peak)
            state[h] = (
                peak,
                old_sum * shrink + summed[:, width:],
                old * shrink + summed[:, :width],
            )
    for h in range(kv_heads):
        _, weight_sum, summed = state[h]
        mixed[:, h] = (summed / weight_sum).reshape(count, group, width)
    staged[...] = mixed[...].reshape(count, heads, width).astype(BF16)
    tail_count = out_ref.shape[1] - count
    copy = pltpu.make_async_copy(staged, out_ref.at[0, pl.ds(tail_count, count)], sem)
    copy.start()
    copy.wait()


def page_attention(queries, state, out, arrived, slots, kv_heads, split):
    count, heads, width = queries.shape
    group = heads // kv_heads
    scale = math.log2(math.e) / math.sqrt(width)
    vmem = pl.BlockSpec(memory_space=pltpu.VMEM)
    hbm = pl.BlockSpec(memory_space=pl.ANY)
    return pl.pallas_call(
        functools.partial(page_kernel, scale, slots, split),
        out_shape=jax.ShapeDtypeStruct(out.shape, BF16),
        in_specs=[vmem] * 4 + [hbm] + [vmem] * len(arrived),
        out_specs=hbm,
        input_output_aliases={4: 0},
        scratch_shapes=[
            pltpu.VMEM((kv_heads, 8 * 64, width), BF16),
            pltpu.VMEM((kv_heads, 8 * 64, width), BF16),
            pltpu.VMEM((count, kv_heads, group, width), F32),
            pltpu.VMEM((count, heads, width), BF16),
            pltpu.SemaphoreType.DMA,
        ],
        compiler_params=pltpu.CompilerParams(vmem_limit_bytes=48 * MIB),
        name="decode_pages",
    )(queries, *state, out, *arrived)


def body(
    request_dest,
    request_slot,
    page_len,
    page_rows,
    kv_cache,
    decode_cache,
    prefix_len,
    cached_len,
    queries,
    fresh_kv,
):
    members = lax.axis_size("inst")
    slots = cached_len.shape[1]
    row_count, heads, width = queries.shape[1:]
    kv_heads = kv_cache.shape[3]
    tail_count = row_count - 2 * slots
    requests, page_depth = page_rows.shape[1:3]
    split = members <= 8
    me = lax.axis_index("inst").astype(jnp.int32)

    pages = page_rows.reshape(requests, page_depth * 2 * kv_heads, width)
    packed = pack(split, members, me.reshape(1), request_dest, request_slot, page_len, pages)
    if split:
        arrived = list(packed)
        for k in range(members - 1, 0, -1):
            arrived[k] = lax.ppermute(packed[k], "inst", [(i, i ^ k) for i in range(members)])
    else:
        arrived = [lax.all_to_all(packed[0], "inst", split_axis=0, concat_axis=0, tiled=True)]

    cache = kv_cache.reshape(-1, width)
    fresh = fresh_kv.reshape(-1, width)
    out = tail_attention(prefix_len, queries, cache, fresh, tail_count, kv_heads)

    step_queries = queries[0, tail_count:]
    own = decode_cache.reshape(-1, width)
    new = fresh[tail_count * 2 * kv_heads :]
    cache_depth = decode_cache.shape[1] // slots
    slot_ids = jnp.arange(slots, dtype=jnp.int32)
    alive = jnp.arange(cache_depth, dtype=jnp.int32)[None, :] < cached_len[0][:, None]
    own_code = jnp.where(alive, slot_ids[:, None], -4 * slots).reshape(-1)
    codes = jnp.concatenate([own_code, slot_ids + slots, slot_ids + 2 * slots])[None, :]
    state = local_state(codes, step_queries, own, new, slots, kv_heads)

    return page_attention(step_queries, state, out, arrived, slots, kv_heads, split)


def solution(mesh):
    placed = (
        P(("groups", "inst"), None),
        P(("groups", "inst"), None),
        P(("groups", "inst"), None),
        P(("groups", "inst"), None, None, None, "tp", None),
        P(("groups", "inst"), None, None, "tp", None),
        P(("groups", "inst"), None, None, "tp", None),
        P(("groups", "inst")),
        P(("groups", "inst"), None),
        P(("groups", "inst"), None, "tp", None),
        P(("groups", "inst"), None, None, "tp", None),
    )
    return jax.shard_map(
        body,
        mesh=mesh,
        in_specs=placed,
        out_specs=P(("groups", "inst"), None, "tp", None),
        check_vma=False,
    )
```

```python
import functools
import math

import jax
import jax.numpy as jnp
from jax import lax
from jax.experimental import pallas as pl
from jax.experimental.pallas import tpu as pltpu
from jax.sharding import PartitionSpec as P

PAIR = 2
NEG = -1e30
F32 = jnp.float32
BF16 = jnp.bfloat16
META = 16
MIB = 1 << 20
LOW, HIGH = 2.0**-40, 2.0**120


def nt_dot(a, b):
    return lax.dot_general(a, b, (((1,), (1,)), ((), ())), preferred_element_type=F32)


def nn_dot(a, b):
    return jnp.dot(a, b, preferred_element_type=F32)


def unmix(kinds, rows):
    keys = rows // kinds
    i = lax.broadcasted_iota(jnp.int32, (rows, rows), 0)
    j = lax.broadcasted_iota(jnp.int32, (rows, rows), 1)
    return jnp.where(j == (i % keys) * kinds + i // keys, 1.0, 0.0).astype(BF16)


def scaled_queries(q, scale):
    q = q * scale
    high = q.astype(BF16)
    low = (q - high.astype(F32)).astype(BF16)
    return jnp.concatenate([high, low], axis=1)


def twice(k):
    return jnp.concatenate([k, k], axis=1)


def with_ones(v):
    return jnp.concatenate([v, jnp.ones_like(v)], axis=1)


def pack_kernel(split, me_ref, dest_hbm, slot_hbm, len_hbm, pages_hbm, *refs):
    *buffers, pages, dest, slot, length, count, table, small_sem, page_sem = refs
    requests, page_rows = pages.shape[:2]
    members = len(buffers) if split else buffers[0].shape[0]
    small = [
        pltpu.make_async_copy(source, target, small_sem.at[i])
        for i, (source, target) in enumerate(
            ((dest_hbm, dest), (slot_hbm, slot), (len_hbm, length))
        )
    ]
    large = pltpu.make_async_copy(pages_hbm, pages, page_sem)
    for copy in small:
        copy.start()
    large.start()

    def clear(k, _):
        count[k] = 0
        for half in range(PAIR):
            table[k * PAIR + half] = -1
        return 0

    lax.fori_loop(0, members, clear, 0)
    for copy in small:
        copy.wait()
    me = me_ref[0]

    def place(r, _):
        peer = dest[0, r] ^ me if split else dest[0, r]
        at = count[peer]
        count[peer] = at + 1
        table[peer * PAIR + at] = r
        return 0

    lax.fori_loop(0, requests, place, 0)
    lane = lax.broadcasted_iota(jnp.int32, (META, 128), 1)
    depth = 128 // (2 * PAIR)
    half_of, key_of = (lane // depth) % PAIR, lane % depth

    def fill(k, buffer):
        code = jnp.full((META, 128), -1.0, F32)
        for half in range(PAIR):
            r = table[k * PAIR + half]
            known = jnp.maximum(r, 0)
            live = jnp.where(r >= 0, length[0, known], 0)
            here = jnp.where(half_of == half, key_of, depth) < live
            code = jnp.where(here, slot[0, known].astype(F32), code)
            buffer[half * page_rows : (half + 1) * page_rows, :] = jnp.where(
                r >= 0, pages[known], jnp.zeros((page_rows, 128), BF16)
            )
        buffer[PAIR * page_rows : PAIR * page_rows + META, :] = code.astype(BF16)

    large.wait()
    if split:
        for k in range(members):
            fill(k, buffers[k])
    else:

        def fill_one(k, _):
            fill(k, buffers[0].at[k])
            return 0

        lax.fori_loop(0, members, fill_one, 0)


def pack(split, members, me, dest, slot, length, pages):
    requests, page_rows = pages.shape[:2]
    rows = PAIR * page_rows + META
    if split:
        out_shape = [jax.ShapeDtypeStruct((rows, 128), BF16)] * members
    else:
        out_shape = [jax.ShapeDtypeStruct((members, rows, 128), BF16)]
    return pl.pallas_call(
        functools.partial(pack_kernel, split),
        out_shape=out_shape,
        in_specs=[pl.BlockSpec(memory_space=pltpu.SMEM)] + [pl.BlockSpec(memory_space=pltpu.HBM)] * 4,
        out_specs=[pl.BlockSpec(memory_space=pltpu.VMEM)] * len(out_shape),
        scratch_shapes=[
            pltpu.VMEM(pages.shape, BF16),
            pltpu.SMEM((1, requests), jnp.int32),
            pltpu.SMEM((1, requests), jnp.int32),
            pltpu.SMEM((1, requests), jnp.int32),
            pltpu.SMEM((members,), jnp.int32),
            pltpu.SMEM((members * PAIR,), jnp.int32),
            pltpu.SemaphoreType.DMA((3,)),
            pltpu.SemaphoreType.DMA,
        ],
        compiler_params=pltpu.CompilerParams(vmem_limit_bytes=32 * MIB),
        name="pack_pages",
    )(me, *(pltpu.with_memory_space_constraint(a, pltpu.HBM) for a in (dest, slot, length, pages)))


def sort_rows(cache_ref, fresh_ref, prefix, keys, values_t):
    kv_heads, total, width = keys.shape
    kinds = 2 * kv_heads
    context = cache_ref.shape[0] // kinds
    order = unmix(kinds, 256)
    depth = 256 // kinds
    many = 4 * depth
    for at in range(0, total, many):
        source, base = (cache_ref, at) if at < context else (fresh_ref, at - context)
        parts = [source[base * kinds + 256 * i : base * kinds + 256 * (i + 1), :] for i in range(4)]
        done = nn_dot(order, jnp.concatenate(parts, axis=1))
        parts = [done[:, i * width : (i + 1) * width] for i in range(4)]
        limit = prefix if at < context else total
        live = at + lax.broadcasted_iota(jnp.int32, (many, width), 0) < limit
        for kind in range(kinds):
            rows = jnp.concatenate([p[kind * depth : (kind + 1) * depth] for p in parts], axis=0)
            rows = jnp.where(live, rows, 0.0).astype(BF16)
            if kind < kv_heads:
                keys[kind, at : at + many, :] = rows
            else:
                values_t[kind - kv_heads, 0:width, at : at + many] = rows.T
    extra = values_t.shape[1] - width
    lane = lax.broadcasted_iota(jnp.int32, (extra, total), 1)
    ones = jnp.where((lane < prefix) | (lane >= context), 1.0, 0.0).astype(BF16)
    for h in range(kv_heads):
        values_t[h, width:, :] = ones


def tail_kernel(scale, slots, near_count, prefix_ref, cached_ref, q_ref, step_q_ref, cache_ref, fresh_ref, own_ref, *refs):
    near = refs[:near_count]
    o_ref, scaled_ref, *state, keys, values_t, mixed, some_keys, some_values = refs[near_count:]
    block, heads, width = q_ref.shape[1:]
    kv_heads, total = keys.shape[:2]
    group = heads // kv_heads
    context = cache_ref.shape[0] // (2 * kv_heads)
    step = pl.program_id(0)
    prefix = prefix_ref[0]

    @pl.when(step == 0)
    def _():
        sort_rows(cache_ref, fresh_ref, prefix, keys, values_t)
        start_decode(
            scale, slots, cached_ref, step_q_ref, own_ref, fresh_ref, total - context, scaled_ref, state, some_keys, some_values
        )
        if near:
            add_pages(slots, group, near, scaled_ref, state, some_keys, some_values)

    rows = block * group
    queries = q_ref[0].astype(F32).reshape(block, kv_heads, group, width)

    def attend(at, exact):
        count = context + (at + 1) * block
        fine = jnp.ones((8, rows), F32)
        for h in range(kv_heads):
            q = scaled_queries(queries[:, h].reshape(rows, width), scale)
            scores = nt_dot(twice(keys[h, :count]), q)
            if exact:
                key = lax.broadcasted_iota(jnp.int32, (count, rows), 0)
                row = lax.broadcasted_iota(jnp.int32, (count, rows), 1) // group
                limit = jnp.where(key < context, prefix, row + (context + at * block + 1))
                scores = jnp.where(key < limit, scores, NEG)
                weights = jnp.exp2(scores - jnp.max(scores, axis=0, keepdims=True))
            else:
                weights = jnp.exp2(scores)
                key = lax.broadcasted_iota(jnp.int32, (block, rows), 0)
                row = lax.broadcasted_iota(jnp.int32, (block, rows), 1) // group
                last = jnp.where(key <= row, weights[count - block :], 0.0)
                weights = jnp.concatenate([weights[: count - block], last], axis=0)
            summed = nn_dot(values_t[h, :, :count], weights.astype(BF16))
            total_weight = summed[width : width + 8]
            fine = jnp.where(
                total_weight >= LOW, jnp.where(total_weight <= HIGH, fine, 0.0), 0.0
            )
            out = summed[:width] / total_weight[0:1]
            mixed[:, h] = out.T.reshape(block, group, width)
        return fine

    for at in range((total - context) // block):

        @pl.when(step == at)
        def _():
            fine = attend(at, False)

            @pl.when(jnp.min(fine) < 0.5)
            def _():
                attend(at, True)

    o_ref[0] = mixed[...].reshape(block, heads, width).astype(BF16)


def tail_attention(prefix, cached, queries, cache, fresh, own, near, tail_count, kv_heads):
    _, row_count, heads, width = queries.shape
    block = min(128, tail_count)
    context = cache.shape[0] // (2 * kv_heads)
    total = context + tail_count
    count = row_count - tail_count
    slots = cached.shape[1]
    rows = count * heads // kv_heads
    local = (own.shape[0] // (2 * kv_heads)) + count
    chunk = max(local, len(near) * PAIR * 32)
    scale = math.log2(math.e) / math.sqrt(width)
    spec = pl.BlockSpec((1, block, heads, width), lambda i: (0, i, 0, 0))
    step_spec = pl.BlockSpec((1, count, heads, width), lambda i: (0, tail_count // count, 0, 0))
    whole = lambda a: pl.BlockSpec(a.shape, lambda i: (0,) * len(a.shape))
    far = lambda a: pltpu.with_memory_space_constraint(a, pltpu.HBM)
    smem = pl.BlockSpec(memory_space=pltpu.SMEM)
    state = jax.ShapeDtypeStruct((kv_heads, rows, width), F32)
    scaled = jax.ShapeDtypeStruct((kv_heads, rows, 2 * width), BF16)
    return pl.pallas_call(
        functools.partial(tail_kernel, scale, slots, len(near)),
        grid=(tail_count // block,),
        out_shape=[jax.ShapeDtypeStruct(queries.shape, BF16), scaled, state, state, state],
        in_specs=[smem, smem, spec, step_spec, whole(cache), whole(fresh), whole(own)] + [whole(a) for a in near],
        out_specs=[spec, whole(scaled), whole(state), whole(state), whole(state)],
        scratch_shapes=[
            pltpu.VMEM((kv_heads, total, width), BF16),
            pltpu.VMEM((kv_heads, width + 16, total), BF16),
            pltpu.VMEM((block, kv_heads, heads // kv_heads, width), F32),
            pltpu.VMEM((kv_heads, chunk, width), BF16),
            pltpu.VMEM((kv_heads, chunk, width), BF16),
        ],
        compiler_params=pltpu.CompilerParams(vmem_limit_bytes=40 * MIB),
        cost_estimate=pl.CostEstimate(
            flops=4 * tail_count * heads * total * width * 4,
            bytes_accessed=8 * MIB,
            transcendentals=tail_count * heads * total,
        ),
        name="tail_attention",
    )(prefix, cached, far(queries), far(queries), far(cache), far(fresh), far(own), *near)


def row_place(rows, columns, group, slots):
    row = lax.broadcasted_iota(jnp.int32, (rows, columns), 0) // group
    return row % slots, row // slots


def split_rows(rows, base, keys, values):
    kv_heads = keys.shape[0]
    depth = rows.shape[0] // (2 * kv_heads)
    for h in range(kv_heads):
        keys[h, base : base + depth, :] = rows[h * depth : (h + 1) * depth]
        values[h, base : base + depth, :] = rows[(kv_heads + h) * depth : (kv_heads + h + 1) * depth]


def start_decode(scale, slots, cached_ref, q_ref, own_ref, fresh_ref, tail_count, scaled_ref, state, keys, values):
    count, heads, width = q_ref.shape[1:]
    kv_heads = keys.shape[0]
    group = heads // kv_heads
    kinds = 2 * kv_heads
    own_count = own_ref.shape[0] // kinds
    total = own_count + count
    chunk = min(256, own_ref.shape[0])
    order = unmix(kinds, chunk)
    for at in range(own_ref.shape[0] // chunk):
        rows = nn_dot(order, own_ref[at * chunk : (at + 1) * chunk, :]).astype(BF16)
        split_rows(rows, at * chunk // kinds, keys, values)
    chunk = min(256, count * kinds)
    order = unmix(kinds, chunk)
    for at in range(count * kinds // chunk):
        begin = tail_count * kinds + at * chunk
        rows = nn_dot(order, fresh_ref[begin : begin + chunk, :]).astype(BF16)
        split_rows(rows, own_count + at * chunk // kinds, keys, values)
    rows = count * group
    key = lax.broadcasted_iota(jnp.int32, (1, total), 1)
    depth = own_count // slots
    code = jnp.where(key < own_count, -1, (key - own_count) % slots)
    for s in range(slots):
        mine = jnp.where(key < own_count, key // depth, -1) == s
        code = jnp.where(mine & (key % depth < cached_ref[0, s]), s, code)
    since = jnp.where(key < own_count, 0, (key - own_count) // slots)
    slot, made = row_place(rows, total, group, slots)
    allowed = (code == slot) & (since <= made)
    queries = q_ref[0].astype(F32).reshape(count, kv_heads, group, width)
    peaks, sums, mixes = state
    for h in range(kv_heads):
        q = scaled_queries(queries[:, h].reshape(rows, width), scale)
        scaled_ref[h] = q
        scores = jnp.where(allowed, nt_dot(q, twice(keys[h, :total])), NEG)
        peak = jnp.max(scores, axis=1, keepdims=True)
        weights = jnp.exp2(scores - peak).astype(BF16)
        summed = nn_dot(weights, with_ones(values[h, :total]))
        peaks[h] = jnp.broadcast_to(peak, (rows, width))
        sums[h] = summed[:, width:]
        mixes[h] = summed[:, :width]


def add_pages(slots, group, buffers, scaled_ref, state, keys, values):
    kv_heads, rows, width = state[0].shape
    kinds = 2 * kv_heads
    page_rows = (buffers[0].shape[0] - META) // PAIR
    depth = page_rows // kinds
    order = unmix(kinds, page_rows)
    lane = lax.broadcasted_iota(jnp.int32, (1, 128), 1)
    codes = []
    for k, buffer in enumerate(buffers):
        both = [buffer[half * page_rows : (half + 1) * page_rows, :] for half in range(PAIR)]
        done = nn_dot(order, jnp.concatenate(both, axis=1)).astype(BF16)
        for half in range(PAIR):
            split_rows(
                done[:, half * width : (half + 1) * width], (PAIR * k + half) * depth, keys, values
            )
        codes.append(buffer[PAIR * page_rows : PAIR * page_rows + META, :].astype(F32)[0:1, :])
    code = jnp.concatenate(
        [jnp.where(lane < 64, codes[k], codes[k + 1]) for k in range(0, len(codes), 2)], axis=1
    )
    total = code.shape[1]
    slot, _ = row_place(rows, total, group, slots)
    allowed = code == slot.astype(F32)
    peaks, sums, mixes = state
    for h in range(kv_heads):
        old_peak = peaks[h]
        scores = jnp.where(allowed, nt_dot(scaled_ref[h], twice(keys[h, :total])), NEG)
        peak = jnp.maximum(old_peak, jnp.max(scores, axis=1, keepdims=True))
        weights = jnp.exp2(scores - peak[:, 0:1]).astype(BF16)
        summed = nn_dot(weights, with_ones(values[h, :total]))
        shrink = jnp.exp2(old_peak - peak)
        peaks[h] = peak
        sums[h] = sums[h] * shrink + summed[:, width:]
        mixes[h] = mixes[h] * shrink + summed[:, :width]


def page_kernel(slots, scaled_ref, m_in, l_in, a_in, out_in, *refs):
    *arrived, out_ref, peaks, sums, mixes, keys, values, mixed, staged, sem = refs
    count, kv_heads, group, width = mixed.shape
    state = (peaks, sums, mixes)
    for kept, given in zip(state, (m_in, l_in, a_in)):
        kept[...] = given[...]
    if len(arrived) > 1:
        add_pages(slots, group, arrived, scaled_ref, state, keys, values)
    else:
        buffers = arrived[0]
        per = keys.shape[1] // 64

        def some(i, _):
            part = [buffers.at[i * per + k] for k in range(per)]
            add_pages(slots, group, part, scaled_ref, state, keys, values)
            return 0

        lax.fori_loop(0, buffers.shape[0] // per, some, 0)
    for h in range(kv_heads):
        mixed[:, h] = (mixes[h] / sums[h]).reshape(count, group, width)
    staged[...] = mixed[...].reshape(staged.shape).astype(BF16)
    tail_count = out_ref.shape[1] - count
    copy = pltpu.make_async_copy(staged, out_ref.at[0, pl.ds(tail_count, count)], sem)
    copy.start()
    copy.wait()


def page_attention(scaled, state, out, arrived, slots):
    kv_heads, rows, width = state[0].shape
    heads = out.shape[2]
    group = heads // kv_heads
    count = rows // group
    chunk = 64 * (len(arrived) if len(arrived) > 1 else 8)
    vmem = pl.BlockSpec(memory_space=pltpu.VMEM)
    hbm = pl.BlockSpec(memory_space=pltpu.HBM)
    return pl.pallas_call(
        functools.partial(page_kernel, slots),
        out_shape=jax.ShapeDtypeStruct(out.shape, BF16),
        in_specs=[vmem] * 4 + [hbm] + [vmem] * len(arrived),
        out_specs=hbm,
        input_output_aliases={4: 0},
        scratch_shapes=[pltpu.VMEM(state[0].shape, F32)] * 3
        + [
            pltpu.VMEM((kv_heads, chunk, width), BF16),
            pltpu.VMEM((kv_heads, chunk, width), BF16),
            pltpu.VMEM((count, kv_heads, group, width), F32),
            pltpu.VMEM((count, heads, width), BF16),
            pltpu.SemaphoreType.DMA,
        ],
        compiler_params=pltpu.CompilerParams(vmem_limit_bytes=48 * MIB),
        name="decode_pages",
    )(scaled, *state, out, *arrived)


def body(
    request_dest,
    request_slot,
    page_len,
    page_rows,
    kv_cache,
    decode_cache,
    prefix_len,
    cached_len,
    queries,
    fresh_kv,
):
    members = lax.axis_size("inst")
    slots = cached_len.shape[1]
    row_count, heads, width = queries.shape[1:]
    kv_heads = kv_cache.shape[3]
    tail_count = row_count - 2 * slots
    requests, page_depth = page_rows.shape[1:3]
    split = members <= 8
    me = lax.axis_index("inst").astype(jnp.int32)

    pages = page_rows.reshape(requests, page_depth * 2 * kv_heads, width)
    packed = pack(split, members, me.reshape(1), request_dest, request_slot, page_len, pages)
    if split:
        half = members // 2
        swap = lambda block, k: lax.ppermute(block, "inst", [(i, i ^ k) for i in range(members)])
        near = [packed[0]] + [swap(packed[k], k) for k in range(1, half)]
        arrived = []
        for k in range(members - 1, half - 1, -1):
            arrived.append(swap(packed[k], k))
    else:
        near = []
        arrived = [lax.all_to_all(packed[0], "inst", split_axis=0, concat_axis=0, tiled=True)]

    out, scaled, *state = tail_attention(
        prefix_len,
        cached_len,
        queries,
        kv_cache.reshape(-1, width),
        fresh_kv.reshape(-1, width),
        decode_cache.reshape(-1, width),
        near,
        tail_count,
        kv_heads,
    )
    return page_attention(scaled, state, out, arrived, slots)


def solution(mesh):
    placed = (
        P(("groups", "inst"), None),
        P(("groups", "inst"), None),
        P(("groups", "inst"), None),
        P(("groups", "inst"), None, None, None, "tp", None),
        P(("groups", "inst"), None, None, "tp", None),
        P(("groups", "inst"), None, None, "tp", None),
        P(("groups", "inst")),
        P(("groups", "inst"), None),
        P(("groups", "inst"), None, "tp", None),
        P(("groups", "inst"), None, None, "tp", None),
    )
    return jax.shard_map(
        body,
        mesh=mesh,
        in_specs=placed,
        out_specs=P(("groups", "inst"), None, "tp", None),
        check_vma=False,
    )
```

```python
import functools
import math

import jax
import jax.numpy as jnp
from jax import lax
from jax.experimental import pallas as pl
from jax.experimental.pallas import tpu as pltpu
from jax.sharding import PartitionSpec as P

PAIR = 2
NEG = -1e30
F32 = jnp.float32
BF16 = jnp.bfloat16
META = 16
MIB = 1 << 20
LOW, HIGH = 2.0**-40, 2.0**120


def nt_dot(a, b):
    return lax.dot_general(a, b, (((1,), (1,)), ((), ())), preferred_element_type=F32)


def nn_dot(a, b):
    return jnp.dot(a, b, preferred_element_type=F32)


def unmix(kinds, rows):
    keys = rows // kinds
    i = lax.broadcasted_iota(jnp.int32, (rows, rows), 0)
    j = lax.broadcasted_iota(jnp.int32, (rows, rows), 1)
    return jnp.where(j == (i % keys) * kinds + i // keys, 1.0, 0.0).astype(BF16)


def scaled_queries(q, scale):
    q = q * scale
    high = q.astype(BF16)
    low = (q - high.astype(F32)).astype(BF16)
    return jnp.concatenate([high, low], axis=1)


def twice(k):
    return jnp.concatenate([k, k], axis=1)


def with_ones(v):
    return jnp.concatenate([v, jnp.ones_like(v)], axis=1)


def pack_kernel(split, me_ref, dest_hbm, slot_hbm, len_hbm, pages_hbm, *refs):
    *buffers, pages, dest, slot, length, count, table, small_sem, page_sem = refs
    requests, page_rows = pages.shape[:2]
    members = len(buffers) if split else buffers[0].shape[0]
    small = [
        pltpu.make_async_copy(source, target, small_sem.at[i])
        for i, (source, target) in enumerate(
            ((dest_hbm, dest), (slot_hbm, slot), (len_hbm, length))
        )
    ]
    large = pltpu.make_async_copy(pages_hbm, pages, page_sem)
    for copy in small:
        copy.start()
    large.start()

    def clear(k, _):
        count[k] = 0
        for half in range(PAIR):
            table[k * PAIR + half] = -1
        return 0

    lax.fori_loop(0, members, clear, 0)
    for copy in small:
        copy.wait()
    me = me_ref[0]

    def place(r, _):
        peer = dest[0, r] ^ me if split else dest[0, r]
        at = count[peer]
        count[peer] = at + 1
        table[peer * PAIR + at] = r
        return 0

    lax.fori_loop(0, requests, place, 0)
    lane = lax.broadcasted_iota(jnp.int32, (META, 128), 1)
    depth = 128 // (2 * PAIR)
    half_of, key_of = (lane // depth) % PAIR, lane % depth

    def fill(k, buffer):
        code = jnp.full((META, 128), -1.0, F32)
        for half in range(PAIR):
            r = table[k * PAIR + half]
            known = jnp.maximum(r, 0)
            live = jnp.where(r >= 0, length[0, known], 0)
            here = jnp.where(half_of == half, key_of, depth) < live
            code = jnp.where(here, slot[0, known].astype(F32), code)
            buffer[half * page_rows : (half + 1) * page_rows, :] = jnp.where(
                r >= 0, pages[known], jnp.zeros((page_rows, 128), BF16)
            )
        buffer[PAIR * page_rows : PAIR * page_rows + META, :] = code.astype(BF16)

    large.wait()
    if split:
        for k in range(members):
            fill(k, buffers[k])
    else:

        def fill_one(k, _):
            fill(k, buffers[0].at[k])
            return 0

        lax.fori_loop(0, members, fill_one, 0)


def pack(split, members, me, dest, slot, length, pages):
    requests, page_rows = pages.shape[:2]
    rows = PAIR * page_rows + META
    if split:
        out_shape = [jax.ShapeDtypeStruct((rows, 128), BF16)] * members
    else:
        out_shape = [jax.ShapeDtypeStruct((members, rows, 128), BF16)]
    return pl.pallas_call(
        functools.partial(pack_kernel, split),
        out_shape=out_shape,
        in_specs=[pl.BlockSpec(memory_space=pltpu.SMEM)] + [pl.BlockSpec(memory_space=pltpu.HBM)] * 4,
        out_specs=[pl.BlockSpec(memory_space=pltpu.VMEM)] * len(out_shape),
        scratch_shapes=[
            pltpu.VMEM(pages.shape, BF16),
            pltpu.SMEM((1, requests), jnp.int32),
            pltpu.SMEM((1, requests), jnp.int32),
            pltpu.SMEM((1, requests), jnp.int32),
            pltpu.SMEM((members,), jnp.int32),
            pltpu.SMEM((members * PAIR,), jnp.int32),
            pltpu.SemaphoreType.DMA((3,)),
            pltpu.SemaphoreType.DMA,
        ],
        compiler_params=pltpu.CompilerParams(vmem_limit_bytes=32 * MIB),
        name="pack_pages",
    )(me, *(pltpu.with_memory_space_constraint(a, pltpu.HBM) for a in (dest, slot, length, pages)))


def sort_some(at, source, order, limit, keys, values_t):
    kv_heads, _, width = keys.shape
    kinds = 2 * kv_heads
    depth = 256 // kinds
    many = source.shape[0] // kinds
    parts = [source[256 * i : 256 * (i + 1), :] for i in range(many // depth)]
    done = nn_dot(order, jnp.concatenate(parts, axis=1))
    parts = [done[:, i * width : (i + 1) * width] for i in range(len(parts))]
    live = at + lax.broadcasted_iota(jnp.int32, (many, width), 0) < limit
    for kind in range(kinds):
        rows = jnp.concatenate([p[kind * depth : (kind + 1) * depth] for p in parts], axis=0)
        rows = jnp.where(live, rows, 0.0).astype(BF16)
        if kind < kv_heads:
            keys[kind, at : at + many, :] = rows
        else:
            values_t[kind - kv_heads, 0:width, at : at + many] = rows.T


def attend(scale, at, exact, context, prefix, q_ref, keys, values_t, mixed, staged, out_ref, sems):
    kv_heads, block, group, width = mixed.shape
    rows = block * group
    count = context + (at + 1) * block
    here = pl.ds(at * block, block)
    fine = jnp.ones((8, rows), F32)
    copies = []
    for h in range(kv_heads):
        q = q_ref[0, here, h * group : (h + 1) * group, :].astype(F32).reshape(rows, width)
        scores = nt_dot(twice(keys[h, :count]), scaled_queries(q, scale))
        key = lax.broadcasted_iota(jnp.int32, (block, rows), 0)
        row = lax.broadcasted_iota(jnp.int32, (block, rows), 1) // group
        if exact:
            dead = lax.broadcasted_iota(jnp.int32, (context, rows), 0) >= prefix
            first = jnp.where(dead, NEG, scores[:context])
            last = jnp.where(key <= row, scores[count - block :], NEG)
            middle = [scores[context : count - block]] if at else []
            scores = jnp.concatenate([first, *middle, last], axis=0)
            weights = jnp.exp2(scores - jnp.max(scores, axis=0, keepdims=True))
        else:
            weights = jnp.exp2(scores)
            last = jnp.where(key <= row, weights[count - block :], 0.0)
            weights = jnp.concatenate([weights[: count - block], last], axis=0)
        summed = nn_dot(values_t[h, :, :count], weights.astype(BF16))
        total_weight = summed[width : width + 8]
        fine = jnp.where(total_weight >= LOW, jnp.where(total_weight <= HIGH, fine, 0.0), 0.0)
        mixed[h] = (summed[:width] / total_weight[0:1]).T.reshape(block, group, width)
        if h % 2:
            some = pl.ds((h - 1) * group, 2 * group)
            staged[here, some, :] = jnp.concatenate([mixed[h - 1], mixed[h]], axis=1).astype(BF16)
            copies.append(
                pltpu.make_async_copy(
                    staged.at[here, some, :], out_ref.at[0, here, some, :], sems.at[at, h // 2]
                )
            )
            copies[-1].start()
    return fine, copies


def sort_kernel(scale, slots, prefix_ref, cached_hbm, q_hbm, cache_hbm, fresh_hbm, own_hbm, *refs):
    keys, values_t, scaled_ref, *state = refs[:6]
    some_keys, some_values, cached, step_q, cache, fresh, own, in_sems, sems = refs[6:]
    count = step_q.shape[0]
    kv_heads, total, width = keys.shape
    kinds = 2 * kv_heads
    context = cache.shape[0] // kinds
    tail_count = total - context
    prefix = prefix_ref[0]
    many = 128 * kinds
    loads = []
    for i in range(in_sems.shape[0]):
        size = cache.shape[0] // in_sems.shape[0]
        part = pl.ds(i * size, size)
        loads.append(pltpu.make_async_copy(cache_hbm.at[part, :], cache.at[part, :], in_sems.at[i]))
    others = [
        pltpu.make_async_copy(fresh_hbm, fresh, sems.at[0]),
        pltpu.make_async_copy(own_hbm, own, sems.at[1]),
        pltpu.make_async_copy(q_hbm.at[0, pl.ds(tail_count, count)], step_q, sems.at[2]),
    ]
    others.append(pltpu.make_async_copy(cached_hbm, cached, sems.at[3]))
    for copy in others + loads:
        copy.start()
    order = unmix(kinds, 256)
    extra = values_t.shape[1] - width
    lane = lax.broadcasted_iota(jnp.int32, (extra, total), 1)
    ones = jnp.where((lane < prefix) | (lane >= context), 1.0, 0.0).astype(BF16)
    for h in range(kv_heads):
        values_t[h, width:, :] = ones
    for copy in others:
        copy.wait()
    start_decode(
        scale, slots, cached, step_q, own, fresh, tail_count, scaled_ref, state, some_keys, some_values
    )
    for i in range(tail_count // 128):
        sort_some(
            context + i * 128, fresh.at[pl.ds(i * many, many), :], order, total, keys, values_t
        )
    per = context // 128 // len(loads)
    for i in range(context // 128):
        if i % per == 0:
            loads[i // per].wait()
        sort_some(i * 128, cache.at[pl.ds(i * many, many), :], order, prefix, keys, values_t)


def far_off(a):
    return pltpu.with_memory_space_constraint(a, pltpu.HBM)


def sort_keys(prefix, cached, queries, cache, fresh, own, tail_count, kv_heads):
    _, row_count, heads, width = queries.shape
    kinds = 2 * kv_heads
    context = cache.shape[0] // kinds
    total = context + tail_count
    count = row_count - tail_count
    rows = count * heads // kv_heads
    local = own.shape[0] // kinds + count
    scale = math.log2(math.e) / math.sqrt(width)
    smem = pl.BlockSpec(memory_space=pltpu.SMEM)
    vmem = pl.BlockSpec(memory_space=pltpu.VMEM)
    hbm = pl.BlockSpec(memory_space=pltpu.HBM)
    state = jax.ShapeDtypeStruct((kv_heads, rows, width), F32)
    return pl.pallas_call(
        functools.partial(sort_kernel, scale, cached.shape[1]),
        out_shape=[
            jax.ShapeDtypeStruct((kv_heads, total, width), BF16),
            jax.ShapeDtypeStruct((kv_heads, width + 16, total), BF16),
            jax.ShapeDtypeStruct((kv_heads, rows, 2 * width), BF16),
            state,
            state,
            state,
        ],
        in_specs=[smem, hbm, hbm, hbm, hbm, hbm],
        out_specs=[vmem] * 6,
        scratch_shapes=[
            pltpu.VMEM((kv_heads, local, width), BF16),
            pltpu.VMEM((kv_heads, local, width), BF16),
            pltpu.SMEM(cached.shape, jnp.int32),
            pltpu.VMEM((count, heads, width), BF16),
            pltpu.VMEM(cache.shape, BF16),
            pltpu.VMEM(fresh.shape, BF16),
            pltpu.VMEM(own.shape, BF16),
            pltpu.SemaphoreType.DMA((1,)),
            pltpu.SemaphoreType.DMA((4,)),
        ],
        compiler_params=pltpu.CompilerParams(vmem_limit_bytes=24 * MIB),
        cost_estimate=pl.CostEstimate(flops=1, bytes_accessed=12 * MIB, transcendentals=0),
        name="sort_keys",
    )(prefix, *(far_off(a) for a in (cached, queries, cache, fresh, own)))


def tail_kernel(scale, context, prefix_ref, q_ref, keys, values_t, out_ref, mixed, staged, sems):
    block = mixed.shape[1]
    prefix = prefix_ref[0]
    results = []
    for at in range(staged.shape[0] // block):
        results.append(
            attend(scale, at, False, context, prefix, q_ref, keys, values_t, mixed, staged, out_ref, sems)
        )
    for at, (fine, copies) in enumerate(results):
        for copy in copies:
            copy.wait()

        @pl.when(jnp.min(fine) < 0.5)
        def _():
            _, again = attend(
                scale, at, True, context, prefix, q_ref, keys, values_t, mixed, staged, out_ref, sems
            )
            for copy in again:
                copy.wait()


def tail_attention(prefix, queries, keys, values_t, tail_count):
    _, row_count, heads, width = queries.shape
    kv_heads, total, _ = keys.shape
    block = min(128, tail_count)
    group = heads // kv_heads
    scale = math.log2(math.e) / math.sqrt(width)
    smem = pl.BlockSpec(memory_space=pltpu.SMEM)
    vmem = pl.BlockSpec(memory_space=pltpu.VMEM)
    hbm = pl.BlockSpec(memory_space=pltpu.HBM)
    return pl.pallas_call(
        functools.partial(tail_kernel, scale, total - tail_count),
        out_shape=jax.ShapeDtypeStruct(queries.shape, BF16),
        in_specs=[smem] + [vmem] * 3,
        out_specs=hbm,
        scratch_shapes=[
            pltpu.VMEM((kv_heads, block, group, width), F32),
            pltpu.VMEM((tail_count, heads, width), BF16),
            pltpu.SemaphoreType.DMA((tail_count // block, kv_heads // 2)),
        ],
        compiler_params=pltpu.CompilerParams(vmem_limit_bytes=36 * MIB),
        cost_estimate=pl.CostEstimate(
            flops=16 * tail_count * heads * total * width,
            bytes_accessed=8 * MIB,
            transcendentals=tail_count * heads * total,
        ),
        name="tail_attention",
    )(prefix, queries, keys, values_t)


def row_place(rows, columns, group, slots):
    row = lax.broadcasted_iota(jnp.int32, (rows, columns), 0) // group
    return row % slots, row // slots


def split_rows(rows, base, keys, values):
    kv_heads = keys.shape[0]
    depth = rows.shape[0] // (2 * kv_heads)
    for h in range(kv_heads):
        keys[h, base : base + depth, :] = rows[h * depth : (h + 1) * depth]
        values[h, base : base + depth, :] = rows[(kv_heads + h) * depth : (kv_heads + h + 1) * depth]


def start_decode(scale, slots, cached_ref, q_ref, own_ref, fresh_ref, tail_count, scaled_ref, state, keys, values):
    count, heads, width = q_ref.shape
    kv_heads = keys.shape[0]
    group = heads // kv_heads
    kinds = 2 * kv_heads
    own_count = own_ref.shape[0] // kinds
    total = own_count + count
    chunk = min(256, own_ref.shape[0])
    order = unmix(kinds, chunk)
    for at in range(own_ref.shape[0] // chunk):
        rows = nn_dot(order, own_ref[at * chunk : (at + 1) * chunk, :]).astype(BF16)
        split_rows(rows, at * chunk // kinds, keys, values)
    chunk = min(256, count * kinds)
    order = unmix(kinds, chunk)
    for at in range(count * kinds // chunk):
        begin = tail_count * kinds + at * chunk
        rows = nn_dot(order, fresh_ref[begin : begin + chunk, :]).astype(BF16)
        split_rows(rows, own_count + at * chunk // kinds, keys, values)
    rows = count * group
    key = lax.broadcasted_iota(jnp.int32, (1, total), 1)
    depth = own_count // slots
    code = jnp.where(key < own_count, -1, (key - own_count) % slots)
    for s in range(slots):
        mine = jnp.where(key < own_count, key // depth, -1) == s
        code = jnp.where(mine & (key % depth < cached_ref[0, s]), s, code)
    since = jnp.where(key < own_count, 0, (key - own_count) // slots)
    slot, made = row_place(rows, total, group, slots)
    allowed = (code == slot) & (since <= made)
    queries = q_ref[...].astype(F32).reshape(count, kv_heads, group, width)
    peaks, sums, mixes = state
    for h in range(kv_heads):
        q = scaled_queries(queries[:, h].reshape(rows, width), scale)
        scaled_ref[h] = q
        scores = jnp.where(allowed, nt_dot(q, twice(keys[h, :total])), NEG)
        peak = jnp.max(scores, axis=1, keepdims=True)
        weights = jnp.exp2(scores - peak).astype(BF16)
        summed = nn_dot(weights, with_ones(values[h, :total]))
        peaks[h] = jnp.broadcast_to(peak, (rows, width))
        sums[h] = summed[:, width:]
        mixes[h] = summed[:, :width]


def add_pages(slots, group, buffers, scaled_ref, state, finish, keys, values, target=None):
    kv_heads, rows, width = state[0].shape
    kinds = 2 * kv_heads
    page_rows = (buffers[0].shape[0] - META) // PAIR
    depth = page_rows // kinds
    order = unmix(kinds, page_rows)
    lane = lax.broadcasted_iota(jnp.int32, (1, 128), 1)
    codes = []
    for k, buffer in enumerate(buffers):
        both = [buffer[half * page_rows : (half + 1) * page_rows, :] for half in range(PAIR)]
        done = nn_dot(order, jnp.concatenate(both, axis=1)).astype(BF16)
        for half in range(PAIR):
            split_rows(
                done[:, half * width : (half + 1) * width], (PAIR * k + half) * depth, keys, values
            )
        codes.append(buffer[PAIR * page_rows : PAIR * page_rows + META, :].astype(F32)[0:1, :])
    code = jnp.concatenate(
        [jnp.where(lane < 64, codes[k], codes[k + 1]) for k in range(0, len(codes), 2)], axis=1
    )
    total = code.shape[1]
    slot, _ = row_place(rows, total, group, slots)
    allowed = code == slot.astype(F32)
    peaks, sums, mixes = state
    for h in range(kv_heads):
        old_peak = peaks[h]
        scores = jnp.where(allowed, nt_dot(scaled_ref[h], twice(keys[h, :total])), NEG)
        peak = jnp.maximum(old_peak, jnp.max(scores, axis=1, keepdims=True))
        weights = jnp.exp2(scores - peak[:, 0:1]).astype(BF16)
        summed = nn_dot(weights, with_ones(values[h, :total]))
        shrink = jnp.exp2(old_peak - peak)
        weight_sum = sums[h] * shrink + summed[:, width:]
        mix = mixes[h] * shrink + summed[:, :width]
        if finish:
            finish(h, weight_sum, mix)
        else:
            for kept, new in zip(target or state, (peak, weight_sum, mix)):
                kept[h] = new


def middle_kernel(slots, group, scaled_ref, m_in, l_in, a_in, *refs):
    *arrived, peaks, sums, mixes, keys, values = refs
    given, state = (m_in, l_in, a_in), (peaks, sums, mixes)
    add_pages(slots, group, arrived, scaled_ref, given, None, keys, values, state)


def middle_pages(scaled, state, arrived, slots, group):
    kv_heads, rows, width = state[0].shape
    vmem = pl.BlockSpec(memory_space=pltpu.VMEM)
    return pl.pallas_call(
        functools.partial(middle_kernel, slots, group),
        out_shape=[jax.ShapeDtypeStruct(state[0].shape, F32)] * 3,
        in_specs=[vmem] * (4 + len(arrived)),
        out_specs=[vmem] * 3,
        scratch_shapes=[pltpu.VMEM((kv_heads, 64 * len(arrived), width), BF16)] * 2,
        compiler_params=pltpu.CompilerParams(vmem_limit_bytes=16 * MIB),
        name="middle_pages",
    )(scaled, *state, *arrived)


def page_kernel(slots, scaled_ref, m_in, l_in, a_in, out_in, *refs):
    *arrived, out_ref, peaks, sums, mixes, keys, values, mixed, staged, sems = refs
    kv_heads, count, group, width = mixed.shape
    given, state = (m_in, l_in, a_in), (peaks, sums, mixes)
    tail_count = out_ref.shape[1] - count
    copies = []

    def finish(h, weight_sum, mix):
        mixed[h] = (mix / weight_sum).reshape(count, group, width)
        if h % 2:
            some = pl.ds((h - 1) * group, 2 * group)
            staged[:, some, :] = jnp.concatenate([mixed[h - 1], mixed[h]], axis=1).astype(BF16)
            copies.append(
                pltpu.make_async_copy(
                    staged.at[:, some, :],
                    out_ref.at[0, pl.ds(tail_count, count), some, :],
                    sems.at[h // 2],
                )
            )
            copies[-1].start()

    if len(arrived) > 1:
        add_pages(slots, group, arrived, scaled_ref, given, finish, keys, values)
    else:
        buffers = arrived[0]
        per = keys.shape[1] // 64
        for kept, old in zip(state, given):
            kept[...] = old[...]

        def some_pages(i, _):
            part = [buffers.at[i * per + k] for k in range(per)]
            add_pages(slots, group, part, scaled_ref, state, None, keys, values)
            return 0

        lax.fori_loop(0, buffers.shape[0] // per, some_pages, 0)
        for h in range(kv_heads):
            finish(h, sums[h], mixes[h])
    for copy in copies:
        copy.wait()


def page_attention(scaled, state, out, arrived, slots):
    kv_heads, rows, width = state[0].shape
    heads = out.shape[2]
    group = heads // kv_heads
    count = rows // group
    chunk = 64 * (len(arrived) if len(arrived) > 1 else 8)
    vmem = pl.BlockSpec(memory_space=pltpu.VMEM)
    hbm = pl.BlockSpec(memory_space=pltpu.HBM)
    return pl.pallas_call(
        functools.partial(page_kernel, slots),
        out_shape=jax.ShapeDtypeStruct(out.shape, BF16),
        in_specs=[vmem] * 4 + [hbm] + [vmem] * len(arrived),
        out_specs=hbm,
        input_output_aliases={4: 0},
        scratch_shapes=[pltpu.VMEM(state[0].shape, F32)] * 3
        + [
            pltpu.VMEM((kv_heads, chunk, width), BF16),
            pltpu.VMEM((kv_heads, chunk, width), BF16),
            pltpu.VMEM((kv_heads, count, group, width), F32),
            pltpu.VMEM((count, heads, width), BF16),
            pltpu.SemaphoreType.DMA((kv_heads // 2,)),
        ],
        compiler_params=pltpu.CompilerParams(vmem_limit_bytes=48 * MIB),
        name="decode_pages",
    )(scaled, *state, out, *arrived)


def body(
    request_dest,
    request_slot,
    page_len,
    page_rows,
    kv_cache,
    decode_cache,
    prefix_len,
    cached_len,
    queries,
    fresh_kv,
):
    members = lax.axis_size("inst")
    slots = cached_len.shape[1]
    row_count, heads, width = queries.shape[1:]
    kv_heads = kv_cache.shape[3]
    tail_count = row_count - 2 * slots
    requests, page_depth = page_rows.shape[1:3]
    split = members <= 8
    me = lax.axis_index("inst").astype(jnp.int32)

    pages = page_rows.reshape(requests, page_depth * 2 * kv_heads, width)
    packed = pack(split, members, me.reshape(1), request_dest, request_slot, page_len, pages)
    keys, values_t, scaled, *state = sort_keys(
        prefix_len,
        cached_len,
        queries,
        kv_cache.reshape(-1, width),
        fresh_kv.reshape(-1, width),
        decode_cache.reshape(-1, width),
        tail_count,
        kv_heads,
    )
    if split:
        half = members // 2
        swap = lambda block, k: lax.ppermute(block, "inst", [(i, i ^ k) for i in range(members)])
        arrived = list(packed)
        for k in [*range(members - 1, members - 3, -1), *range(1, half)]:
            arrived[k] = swap(packed[k], k)
        later = range(half, members - 2)
        keys, arrived[-1], *blocks = lax.optimization_barrier(
            (keys, arrived[-1], *(packed[k] for k in later))
        )
        for k, block in zip(later, blocks):
            arrived[k] = swap(block, k)
    else:
        arrived = [lax.all_to_all(packed[0], "inst", split_axis=0, concat_axis=0, tiled=True)]
    out = tail_attention(prefix_len, queries, keys, values_t, tail_count)
    if split:
        out, *state = lax.optimization_barrier((out, *state))
        first = arrived[:half] + arrived[: half + 1 : -1]
        state = middle_pages(scaled, state, first, slots, heads // kv_heads)
        arrived = arrived[half + 1 : half - 1 : -1]
    return page_attention(scaled, state, out, arrived, slots)


def solution(mesh):
    placed = (
        P(("groups", "inst"), None),
        P(("groups", "inst"), None),
        P(("groups", "inst"), None),
        P(("groups", "inst"), None, None, None, "tp", None),
        P(("groups", "inst"), None, None, "tp", None),
        P(("groups", "inst"), None, None, "tp", None),
        P(("groups", "inst")),
        P(("groups", "inst"), None),
        P(("groups", "inst"), None, "tp", None),
        P(("groups", "inst"), None, None, "tp", None),
    )
    return jax.shard_map(
        body,
        mesh=mesh,
        in_specs=placed,
        out_specs=P(("groups", "inst"), None, "tp", None),
        check_vma=False,
    )
```

```python
import functools
import math

import jax
import jax.numpy as jnp
from jax import lax
from jax.experimental import pallas as pl
from jax.experimental.pallas import tpu as pltpu
from jax.sharding import PartitionSpec as P

PAIR = 2
NEG = -1e30
F32 = jnp.float32
BF16 = jnp.bfloat16
META = 16
MIB = 1 << 20
FAR_ORDER = (0, 2, 1, 3)
LOW, HIGH = 2.0**-40, 2.0**120


def nt_dot(a, b):
    return lax.dot_general(a, b, (((1,), (1,)), ((), ())), preferred_element_type=F32)


def nn_dot(a, b):
    return jnp.dot(a, b, preferred_element_type=F32)


def unmix(kinds, rows):
    keys = rows // kinds
    i = lax.broadcasted_iota(jnp.int32, (rows, rows), 0)
    j = lax.broadcasted_iota(jnp.int32, (rows, rows), 1)
    return jnp.where(j == (i % keys) * kinds + i // keys, 1.0, 0.0).astype(BF16)


def scaled_queries(q, scale):
    q = q * scale
    high = q.astype(BF16)
    low = (q - high.astype(F32)).astype(BF16)
    return jnp.concatenate([high, low], axis=1)


def twice(k):
    return jnp.concatenate([k, k], axis=1)


def with_ones(v):
    return jnp.concatenate([v, jnp.ones_like(v)], axis=1)


def pack_kernel(split, me_ref, dest_hbm, slot_hbm, len_hbm, pages_hbm, *refs):
    *buffers, pages, dest, slot, length, count, table, small_sem, page_sem = refs
    requests, page_rows = pages.shape[:2]
    members = len(buffers) if split else buffers[0].shape[0]
    small = [
        pltpu.make_async_copy(source, target, small_sem.at[i])
        for i, (source, target) in enumerate(
            ((dest_hbm, dest), (slot_hbm, slot), (len_hbm, length))
        )
    ]
    large = pltpu.make_async_copy(pages_hbm, pages, page_sem)
    for copy in small:
        copy.start()
    large.start()

    def clear(k, _):
        count[k] = 0
        for half in range(PAIR):
            table[k * PAIR + half] = -1
        return 0

    lax.fori_loop(0, members, clear, 0)
    for copy in small:
        copy.wait()
    me = me_ref[0]

    def place(r, _):
        peer = dest[0, r] ^ me if split else dest[0, r]
        at = count[peer]
        count[peer] = at + 1
        table[peer * PAIR + at] = r
        return 0

    lax.fori_loop(0, requests, place, 0)
    lane = lax.broadcasted_iota(jnp.int32, (META, 128), 1)
    depth = 128 // (2 * PAIR)
    half_of, key_of = (lane // depth) % PAIR, lane % depth

    def fill(k, buffer):
        code = jnp.full((META, 128), -1.0, F32)
        for half in range(PAIR):
            r = table[k * PAIR + half]
            known = jnp.maximum(r, 0)
            live = jnp.where(r >= 0, length[0, known], 0)
            here = jnp.where(half_of == half, key_of, depth) < live
            code = jnp.where(here, slot[0, known].astype(F32), code)
            buffer[half * page_rows : (half + 1) * page_rows, :] = jnp.where(
                r >= 0, pages[known], jnp.zeros((page_rows, 128), BF16)
            )
        buffer[PAIR * page_rows : PAIR * page_rows + META, :] = code.astype(BF16)

    large.wait()
    if split:
        for k in range(members):
            fill(k, buffers[k])
    else:

        def fill_one(k, _):
            fill(k, buffers[0].at[k])
            return 0

        lax.fori_loop(0, members, fill_one, 0)


def pack(split, members, me, dest, slot, length, pages):
    requests, page_rows = pages.shape[:2]
    rows = PAIR * page_rows + META
    if split:
        out_shape = [jax.ShapeDtypeStruct((rows, 128), BF16)] * members
    else:
        out_shape = [jax.ShapeDtypeStruct((members, rows, 128), BF16)]
    return pl.pallas_call(
        functools.partial(pack_kernel, split),
        out_shape=out_shape,
        in_specs=[pl.BlockSpec(memory_space=pltpu.SMEM)] + [pl.BlockSpec(memory_space=pltpu.HBM)] * 4,
        out_specs=[pl.BlockSpec(memory_space=pltpu.VMEM)] * len(out_shape),
        scratch_shapes=[
            pltpu.VMEM(pages.shape, BF16),
            pltpu.SMEM((1, requests), jnp.int32),
            pltpu.SMEM((1, requests), jnp.int32),
            pltpu.SMEM((1, requests), jnp.int32),
            pltpu.SMEM((members,), jnp.int32),
            pltpu.SMEM((members * PAIR,), jnp.int32),
            pltpu.SemaphoreType.DMA((3,)),
            pltpu.SemaphoreType.DMA,
        ],
        compiler_params=pltpu.CompilerParams(vmem_limit_bytes=32 * MIB),
        name="pack_pages",
    )(me, *(pltpu.with_memory_space_constraint(a, pltpu.HBM) for a in (dest, slot, length, pages)))


def sort_some(at, source, order, limit, keys, values_t):
    kv_heads, _, width = keys.shape
    kinds = 2 * kv_heads
    depth = 256 // kinds
    many = source.shape[0] // kinds
    parts = [source[256 * i : 256 * (i + 1), :] for i in range(many // depth)]
    done = nn_dot(order, jnp.concatenate(parts, axis=1))
    parts = [done[:, i * width : (i + 1) * width] for i in range(len(parts))]
    live = at + lax.broadcasted_iota(jnp.int32, (many, width), 0) < limit
    for kind in range(kinds):
        rows = jnp.concatenate([p[kind * depth : (kind + 1) * depth] for p in parts], axis=0)
        rows = jnp.where(live, rows, 0.0).astype(BF16)
        if kind < kv_heads:
            keys[kind, at : at + many, :] = rows
        else:
            values_t[kind - kv_heads, 0:width, at : at + many] = rows.T


def attend(scale, at, exact, context, prefix, q_ref, keys, values_t, mixed, staged, out_ref, sems):
    kv_heads, block, group, width = mixed.shape
    rows = block * group
    count = context + (at + 1) * block
    here = pl.ds(at * block, block)
    fine = jnp.ones((8, rows), F32)
    copies = []
    for h in range(kv_heads):
        q = q_ref[0, here, h * group : (h + 1) * group, :].astype(F32).reshape(rows, width)
        scores = nt_dot(twice(keys[h, :count]), scaled_queries(q, scale))
        key = lax.broadcasted_iota(jnp.int32, (block, rows), 0)
        row = lax.broadcasted_iota(jnp.int32, (block, rows), 1) // group
        if exact:
            dead = lax.broadcasted_iota(jnp.int32, (context, rows), 0) >= prefix
            first = jnp.where(dead, NEG, scores[:context])
            last = jnp.where(key <= row, scores[count - block :], NEG)
            middle = [scores[context : count - block]] if at else []
            scores = jnp.concatenate([first, *middle, last], axis=0)
            weights = jnp.exp2(scores - jnp.max(scores, axis=0, keepdims=True))
        else:
            weights = jnp.exp2(scores)
            last = jnp.where(key <= row, weights[count - block :], 0.0)
            weights = jnp.concatenate([weights[: count - block], last], axis=0)
        summed = nn_dot(values_t[h, :, :count], weights.astype(BF16))
        total_weight = summed[width : width + 8]
        fine = jnp.where(total_weight >= LOW, jnp.where(total_weight <= HIGH, fine, 0.0), 0.0)
        mixed[h] = (summed[:width] / total_weight[0:1]).T.reshape(block, group, width)
        if h % 2:
            some = pl.ds((h - 1) * group, 2 * group)
            staged[here, some, :] = jnp.concatenate([mixed[h - 1], mixed[h]], axis=1).astype(BF16)
            copies.append(
                pltpu.make_async_copy(
                    staged.at[here, some, :], out_ref.at[0, here, some, :], sems.at[at, h // 2]
                )
            )
            copies[-1].start()
    return fine, copies


def sort_kernel(scale, slots, prefix_ref, cached_hbm, q_hbm, cache_hbm, fresh_hbm, own_hbm, *refs):
    keys, values_t, scaled_ref, *state = refs[:6]
    some_keys, some_values, cached, step_q, cache, fresh, own, in_sems, sems = refs[6:]
    count = step_q.shape[0]
    kv_heads, total, width = keys.shape
    kinds = 2 * kv_heads
    context = cache.shape[0] // kinds
    tail_count = total - context
    prefix = prefix_ref[0]
    many = 128 * kinds
    loads = []
    for i in range(in_sems.shape[0]):
        size = cache.shape[0] // in_sems.shape[0]
        part = pl.ds(i * size, size)
        loads.append(pltpu.make_async_copy(cache_hbm.at[part, :], cache.at[part, :], in_sems.at[i]))
    others = [
        pltpu.make_async_copy(fresh_hbm, fresh, sems.at[0]),
        pltpu.make_async_copy(own_hbm, own, sems.at[1]),
        pltpu.make_async_copy(q_hbm.at[0, pl.ds(tail_count, count)], step_q, sems.at[2]),
    ]
    others.append(pltpu.make_async_copy(cached_hbm, cached, sems.at[3]))
    for copy in others + loads:
        copy.start()
    order = unmix(kinds, 256)
    extra = values_t.shape[1] - width
    lane = lax.broadcasted_iota(jnp.int32, (extra, total), 1)
    ones = jnp.where((lane < prefix) | (lane >= context), 1.0, 0.0).astype(BF16)
    for h in range(kv_heads):
        values_t[h, width:, :] = ones
    for copy in others:
        copy.wait()
    start_decode(
        scale, slots, cached, step_q, own, fresh, tail_count, scaled_ref, state, some_keys, some_values
    )
    for i in range(tail_count // 128):
        sort_some(
            context + i * 128, fresh.at[pl.ds(i * many, many), :], order, total, keys, values_t
        )
    per = context // 128 // len(loads)
    for i in range(context // 128):
        if i % per == 0:
            loads[i // per].wait()
        sort_some(i * 128, cache.at[pl.ds(i * many, many), :], order, prefix, keys, values_t)


def far_off(a):
    return pltpu.with_memory_space_constraint(a, pltpu.HBM)


def sort_keys(prefix, cached, queries, cache, fresh, own, tail_count, kv_heads):
    _, row_count, heads, width = queries.shape
    kinds = 2 * kv_heads
    context = cache.shape[0] // kinds
    total = context + tail_count
    count = row_count - tail_count
    rows = count * heads // kv_heads
    local = own.shape[0] // kinds + count
    scale = math.log2(math.e) / math.sqrt(width)
    smem = pl.BlockSpec(memory_space=pltpu.SMEM)
    vmem = pl.BlockSpec(memory_space=pltpu.VMEM)
    hbm = pl.BlockSpec(memory_space=pltpu.HBM)
    state = jax.ShapeDtypeStruct((kv_heads, rows, width), F32)
    return pl.pallas_call(
        functools.partial(sort_kernel, scale, cached.shape[1]),
        out_shape=[
            jax.ShapeDtypeStruct((kv_heads, total, width), BF16),
            jax.ShapeDtypeStruct((kv_heads, width + 16, total), BF16),
            jax.ShapeDtypeStruct((kv_heads, rows, 2 * width), BF16),
            state,
            state,
            state,
        ],
        in_specs=[smem, hbm, hbm, hbm, hbm, hbm],
        out_specs=[vmem] * 6,
        scratch_shapes=[
            pltpu.VMEM((kv_heads, local, width), BF16),
            pltpu.VMEM((kv_heads, local, width), BF16),
            pltpu.SMEM(cached.shape, jnp.int32),
            pltpu.VMEM((count, heads, width), BF16),
            pltpu.VMEM(cache.shape, BF16),
            pltpu.VMEM(fresh.shape, BF16),
            pltpu.VMEM(own.shape, BF16),
            pltpu.SemaphoreType.DMA((1,)),
            pltpu.SemaphoreType.DMA((4,)),
        ],
        compiler_params=pltpu.CompilerParams(vmem_limit_bytes=24 * MIB),
        cost_estimate=pl.CostEstimate(flops=1, bytes_accessed=12 * MIB, transcendentals=0),
        name="sort_keys",
    )(prefix, *(far_off(a) for a in (cached, queries, cache, fresh, own)))


def tail_kernel(scale, context, prefix_ref, q_ref, keys, values_t, out_ref, mixed, staged, sems):
    block = mixed.shape[1]
    prefix = prefix_ref[0]
    results = []
    for at in range(staged.shape[0] // block):
        results.append(
            attend(scale, at, False, context, prefix, q_ref, keys, values_t, mixed, staged, out_ref, sems)
        )
    for at, (fine, copies) in enumerate(results):
        for copy in copies:
            copy.wait()

        @pl.when(jnp.min(fine) < 0.5)
        def _():
            _, again = attend(
                scale, at, True, context, prefix, q_ref, keys, values_t, mixed, staged, out_ref, sems
            )
            for copy in again:
                copy.wait()


def tail_attention(prefix, queries, keys, values_t, tail_count):
    _, row_count, heads, width = queries.shape
    kv_heads, total, _ = keys.shape
    block = min(128, tail_count)
    group = heads // kv_heads
    scale = math.log2(math.e) / math.sqrt(width)
    smem = pl.BlockSpec(memory_space=pltpu.SMEM)
    vmem = pl.BlockSpec(memory_space=pltpu.VMEM)
    hbm = pl.BlockSpec(memory_space=pltpu.HBM)
    return pl.pallas_call(
        functools.partial(tail_kernel, scale, total - tail_count),
        out_shape=jax.ShapeDtypeStruct(queries.shape, BF16),
        in_specs=[smem] + [vmem] * 3,
        out_specs=hbm,
        scratch_shapes=[
            pltpu.VMEM((kv_heads, block, group, width), F32),
            pltpu.VMEM((tail_count, heads, width), BF16),
            pltpu.SemaphoreType.DMA((tail_count // block, kv_heads // 2)),
        ],
        compiler_params=pltpu.CompilerParams(vmem_limit_bytes=36 * MIB),
        cost_estimate=pl.CostEstimate(
            flops=16 * tail_count * heads * total * width,
            bytes_accessed=8 * MIB,
            transcendentals=tail_count * heads * total,
        ),
        name="tail_attention",
    )(prefix, queries, keys, values_t)


def row_place(rows, columns, group, slots):
    row = lax.broadcasted_iota(jnp.int32, (rows, columns), 0) // group
    return row % slots, row // slots


def split_rows(rows, base, keys, values):
    kv_heads = keys.shape[0]
    depth = rows.shape[0] // (2 * kv_heads)
    for h in range(kv_heads):
        keys[h, base : base + depth, :] = rows[h * depth : (h + 1) * depth]
        values[h, base : base + depth, :] = rows[(kv_heads + h) * depth : (kv_heads + h + 1) * depth]


def start_decode(scale, slots, cached_ref, q_ref, own_ref, fresh_ref, tail_count, scaled_ref, state, keys, values):
    count, heads, width = q_ref.shape
    kv_heads = keys.shape[0]
    group = heads // kv_heads
    kinds = 2 * kv_heads
    own_count = own_ref.shape[0] // kinds
    total = own_count + count
    chunk = min(256, own_ref.shape[0])
    order = unmix(kinds, chunk)
    for at in range(own_ref.shape[0] // chunk):
        rows = nn_dot(order, own_ref[at * chunk : (at + 1) * chunk, :]).astype(BF16)
        split_rows(rows, at * chunk // kinds, keys, values)
    chunk = min(256, count * kinds)
    order = unmix(kinds, chunk)
    for at in range(count * kinds // chunk):
        begin = tail_count * kinds + at * chunk
        rows = nn_dot(order, fresh_ref[begin : begin + chunk, :]).astype(BF16)
        split_rows(rows, own_count + at * chunk // kinds, keys, values)
    rows = count * group
    key = lax.broadcasted_iota(jnp.int32, (1, total), 1)
    depth = own_count // slots
    code = jnp.where(key < own_count, -1, (key - own_count) % slots)
    for s in range(slots):
        mine = jnp.where(key < own_count, key // depth, -1) == s
        code = jnp.where(mine & (key % depth < cached_ref[0, s]), s, code)
    since = jnp.where(key < own_count, 0, (key - own_count) // slots)
    slot, made = row_place(rows, total, group, slots)
    allowed = (code == slot) & (since <= made)
    queries = q_ref[...].astype(F32).reshape(count, kv_heads, group, width)
    peaks, sums, mixes = state
    for h in range(kv_heads):
        q = scaled_queries(queries[:, h].reshape(rows, width), scale)
        scaled_ref[h] = q
        scores = jnp.where(allowed, nt_dot(q, twice(keys[h, :total])), NEG)
        peak = jnp.max(scores, axis=1, keepdims=True)
        weights = jnp.exp2(scores - peak).astype(BF16)
        summed = nn_dot(weights, with_ones(values[h, :total]))
        peaks[h] = jnp.broadcast_to(peak, (rows, width))
        sums[h] = summed[:, width:]
        mixes[h] = summed[:, :width]


def add_pages(slots, group, buffers, scaled_ref, state, finish, keys, values, target=None):
    kv_heads, rows, width = state[0].shape
    kinds = 2 * kv_heads
    page_rows = (buffers[0].shape[0] - META) // PAIR
    depth = page_rows // kinds
    order = unmix(kinds, page_rows)
    lane = lax.broadcasted_iota(jnp.int32, (1, 128), 1)
    codes = []
    for k, buffer in enumerate(buffers):
        both = [buffer[half * page_rows : (half + 1) * page_rows, :] for half in range(PAIR)]
        done = nn_dot(order, jnp.concatenate(both, axis=1)).astype(BF16)
        for half in range(PAIR):
            split_rows(
                done[:, half * width : (half + 1) * width], (PAIR * k + half) * depth, keys, values
            )
        codes.append(buffer[PAIR * page_rows : PAIR * page_rows + META, :].astype(F32)[0:1, :])
    code = jnp.concatenate(
        [jnp.where(lane < 64, codes[k], codes[k + 1]) for k in range(0, len(codes), 2)], axis=1
    )
    total = code.shape[1]
    slot, _ = row_place(rows, total, group, slots)
    allowed = code == slot.astype(F32)
    peaks, sums, mixes = state
    for h in range(kv_heads):
        old_peak = peaks[h]
        scores = jnp.where(allowed, nt_dot(scaled_ref[h], twice(keys[h, :total])), NEG)
        peak = jnp.maximum(old_peak, jnp.max(scores, axis=1, keepdims=True))
        weights = jnp.exp2(scores - peak[:, 0:1]).astype(BF16)
        summed = nn_dot(weights, with_ones(values[h, :total]))
        shrink = jnp.exp2(old_peak - peak)
        weight_sum = sums[h] * shrink + summed[:, width:]
        mix = mixes[h] * shrink + summed[:, :width]
        if finish:
            finish(h, weight_sum, mix)
        else:
            for kept, new in zip(target or state, (peak, weight_sum, mix)):
                kept[h] = new


def middle_kernel(slots, group, scaled_ref, m_in, l_in, a_in, *refs):
    *arrived, peaks, sums, mixes, keys, values = refs
    given, state = (m_in, l_in, a_in), (peaks, sums, mixes)
    add_pages(slots, group, arrived, scaled_ref, given, None, keys, values, state)


def middle_pages(scaled, state, arrived, slots, group):
    kv_heads, rows, width = state[0].shape
    vmem = pl.BlockSpec(memory_space=pltpu.VMEM)
    return pl.pallas_call(
        functools.partial(middle_kernel, slots, group),
        out_shape=[jax.ShapeDtypeStruct(state[0].shape, F32)] * 3,
        in_specs=[vmem] * (4 + len(arrived)),
        out_specs=[vmem] * 3,
        scratch_shapes=[pltpu.VMEM((kv_heads, 64 * len(arrived), width), BF16)] * 2,
        compiler_params=pltpu.CompilerParams(vmem_limit_bytes=16 * MIB),
        name="middle_pages",
    )(scaled, *state, *arrived)


def page_kernel(slots, scaled_ref, m_in, l_in, a_in, out_in, *refs):
    *arrived, out_ref, peaks, sums, mixes, keys, values, mixed, staged, sems = refs
    kv_heads, count, group, width = mixed.shape
    given, state = (m_in, l_in, a_in), (peaks, sums, mixes)
    tail_count = out_ref.shape[1] - count
    copies = []

    def finish(h, weight_sum, mix):
        mixed[h] = (mix / weight_sum).reshape(count, group, width)
        if h % 2:
            some = pl.ds((h - 1) * group, 2 * group)
            staged[:, some, :] = jnp.concatenate([mixed[h - 1], mixed[h]], axis=1).astype(BF16)
            copies.append(
                pltpu.make_async_copy(
                    staged.at[:, some, :],
                    out_ref.at[0, pl.ds(tail_count, count), some, :],
                    sems.at[h // 2],
                )
            )
            copies[-1].start()

    if len(arrived) > 1:
        add_pages(slots, group, arrived, scaled_ref, given, finish, keys, values)
    else:
        buffers = arrived[0]
        per = keys.shape[1] // 64
        for kept, old in zip(state, given):
            kept[...] = old[...]

        def some_pages(i, _):
            part = [buffers.at[i * per + k] for k in range(per)]
            add_pages(slots, group, part, scaled_ref, state, None, keys, values)
            return 0

        lax.fori_loop(0, buffers.shape[0] // per, some_pages, 0)
        for h in range(kv_heads):
            finish(h, sums[h], mixes[h])
    for copy in copies:
        copy.wait()


def page_attention(scaled, state, out, arrived, slots):
    kv_heads, rows, width = state[0].shape
    heads = out.shape[2]
    group = heads // kv_heads
    count = rows // group
    chunk = 64 * (len(arrived) if len(arrived) > 1 else 8)
    vmem = pl.BlockSpec(memory_space=pltpu.VMEM)
    hbm = pl.BlockSpec(memory_space=pltpu.HBM)
    return pl.pallas_call(
        functools.partial(page_kernel, slots),
        out_shape=jax.ShapeDtypeStruct(out.shape, BF16),
        in_specs=[vmem] * 4 + [hbm] + [vmem] * len(arrived),
        out_specs=hbm,
        input_output_aliases={4: 0},
        scratch_shapes=[pltpu.VMEM(state[0].shape, F32)] * 3
        + [
            pltpu.VMEM((kv_heads, chunk, width), BF16),
            pltpu.VMEM((kv_heads, chunk, width), BF16),
            pltpu.VMEM((kv_heads, count, group, width), F32),
            pltpu.VMEM((count, heads, width), BF16),
            pltpu.SemaphoreType.DMA((kv_heads // 2,)),
        ],
        compiler_params=pltpu.CompilerParams(vmem_limit_bytes=48 * MIB),
        name="decode_pages",
    )(scaled, *state, out, *arrived)


def body(
    request_dest,
    request_slot,
    page_len,
    page_rows,
    kv_cache,
    decode_cache,
    prefix_len,
    cached_len,
    queries,
    fresh_kv,
):
    members = lax.axis_size("inst")
    slots = cached_len.shape[1]
    row_count, heads, width = queries.shape[1:]
    kv_heads = kv_cache.shape[3]
    tail_count = row_count - 2 * slots
    requests, page_depth = page_rows.shape[1:3]
    split = members <= 8
    me = lax.axis_index("inst").astype(jnp.int32)

    pages = page_rows.reshape(requests, page_depth * 2 * kv_heads, width)
    packed = pack(split, members, me.reshape(1), request_dest, request_slot, page_len, pages)
    keys, values_t, scaled, *state = sort_keys(
        prefix_len,
        cached_len,
        queries,
        kv_cache.reshape(-1, width),
        fresh_kv.reshape(-1, width),
        decode_cache.reshape(-1, width),
        tail_count,
        kv_heads,
    )
    if split:
        half = members // 2
        far = [half + i for i in FAR_ORDER] if half == len(FAR_ORDER) else list(range(half, members))
        swap = lambda block, k: lax.ppermute(block, "inst", [(i, i ^ k) for i in range(members)])
        arrived = list(packed)
        for k in [*far[: half - 2], *range(1, half)]:
            arrived[k] = swap(packed[k], k)
        later = far[half - 2 :]
        keys, arrived[far[0]], *blocks = lax.optimization_barrier(
            (keys, arrived[far[0]], *(packed[k] for k in later))
        )
        for k, block in zip(later, blocks):
            arrived[k] = swap(block, k)
    else:
        arrived = [lax.all_to_all(packed[0], "inst", split_axis=0, concat_axis=0, tiled=True)]
    out = tail_attention(prefix_len, queries, keys, values_t, tail_count)
    if split:
        out, *state = lax.optimization_barrier((out, *state))
        first = arrived[:half] + [arrived[k] for k in far[: half - 2]]
        state = middle_pages(scaled, state, first, slots, heads // kv_heads)
        arrived = [arrived[k] for k in later]
    return page_attention(scaled, state, out, arrived, slots)


def solution(mesh):
    placed = (
        P(("groups", "inst"), None),
        P(("groups", "inst"), None),
        P(("groups", "inst"), None),
        P(("groups", "inst"), None, None, None, "tp", None),
        P(("groups", "inst"), None, None, "tp", None),
        P(("groups", "inst"), None, None, "tp", None),
        P(("groups", "inst")),
        P(("groups", "inst"), None),
        P(("groups", "inst"), None, "tp", None),
        P(("groups", "inst"), None, None, "tp", None),
    )
    return jax.shard_map(
        body,
        mesh=mesh,
        in_specs=placed,
        out_specs=P(("groups", "inst"), None, "tp", None),
        check_vma=False,
    )
```

```python
import functools
import math

import jax
import jax.numpy as jnp
from jax import lax
from jax.experimental import pallas as pl
from jax.experimental.pallas import tpu as pltpu
from jax.sharding import PartitionSpec as P

PAIR = 2
NEG = -1e30
F32 = jnp.float32
BF16 = jnp.bfloat16
META = 16
MIB = 1 << 20
FAR_ORDER = (0, 3, 1, 2)
LOW, HIGH = 2.0**-40, 2.0**120


def nt_dot(a, b):
    return lax.dot_general(a, b, (((1,), (1,)), ((), ())), preferred_element_type=F32)


def nn_dot(a, b):
    return jnp.dot(a, b, preferred_element_type=F32)


def unmix(kinds, rows):
    keys = rows // kinds
    i = lax.broadcasted_iota(jnp.int32, (rows, rows), 0)
    j = lax.broadcasted_iota(jnp.int32, (rows, rows), 1)
    return jnp.where(j == (i % keys) * kinds + i // keys, 1.0, 0.0).astype(BF16)


def scaled_queries(q, scale):
    q = q * scale
    high = q.astype(BF16)
    low = (q - high.astype(F32)).astype(BF16)
    return jnp.concatenate([high, low], axis=1)


def twice(k):
    return jnp.concatenate([k, k], axis=1)


def with_ones(v):
    return jnp.concatenate([v, jnp.ones_like(v)], axis=1)


def pack_kernel(split, me_ref, dest_hbm, slot_hbm, len_hbm, pages_hbm, *refs):
    *buffers, pages, dest, slot, length, count, table, small_sem, page_sem = refs
    requests, page_rows = pages.shape[:2]
    members = len(buffers) if split else buffers[0].shape[0]
    small = [
        pltpu.make_async_copy(source, target, small_sem.at[i])
        for i, (source, target) in enumerate(
            ((dest_hbm, dest), (slot_hbm, slot), (len_hbm, length))
        )
    ]
    large = pltpu.make_async_copy(pages_hbm, pages, page_sem)
    for copy in small:
        copy.start()
    large.start()

    def clear(k, _):
        count[k] = 0
        for half in range(PAIR):
            table[k * PAIR + half] = -1
        return 0

    lax.fori_loop(0, members, clear, 0)
    for copy in small:
        copy.wait()
    me = me_ref[0]

    def place(r, _):
        peer = dest[0, r] ^ me if split else dest[0, r]
        at = count[peer]
        count[peer] = at + 1
        table[peer * PAIR + at] = r
        return 0

    lax.fori_loop(0, requests, place, 0)
    lane = lax.broadcasted_iota(jnp.int32, (META, 128), 1)
    depth = 128 // (2 * PAIR)
    half_of, key_of = (lane // depth) % PAIR, lane % depth

    def fill(k, buffer):
        code = jnp.full((META, 128), -1.0, F32)
        for half in range(PAIR):
            r = table[k * PAIR + half]
            known = jnp.maximum(r, 0)
            live = jnp.where(r >= 0, length[0, known], 0)
            here = jnp.where(half_of == half, key_of, depth) < live
            code = jnp.where(here, slot[0, known].astype(F32), code)
            buffer[half * page_rows : (half + 1) * page_rows, :] = jnp.where(
                r >= 0, pages[known], jnp.zeros((page_rows, 128), BF16)
            )
        buffer[PAIR * page_rows : PAIR * page_rows + META, :] = code.astype(BF16)

    large.wait()
    if split:
        for k in range(members):
            fill(k, buffers[k])
    else:

        def fill_one(k, _):
            fill(k, buffers[0].at[k])
            return 0

        lax.fori_loop(0, members, fill_one, 0)


def pack(split, members, me, dest, slot, length, pages):
    requests, page_rows = pages.shape[:2]
    rows = PAIR * page_rows + META
    if split:
        out_shape = [jax.ShapeDtypeStruct((rows, 128), BF16)] * members
    else:
        out_shape = [jax.ShapeDtypeStruct((members, rows, 128), BF16)]
    return pl.pallas_call(
        functools.partial(pack_kernel, split),
        out_shape=out_shape,
        in_specs=[pl.BlockSpec(memory_space=pltpu.SMEM)] + [pl.BlockSpec(memory_space=pltpu.HBM)] * 4,
        out_specs=[pl.BlockSpec(memory_space=pltpu.VMEM)] * len(out_shape),
        scratch_shapes=[
            pltpu.VMEM(pages.shape, BF16),
            pltpu.SMEM((1, requests), jnp.int32),
            pltpu.SMEM((1, requests), jnp.int32),
            pltpu.SMEM((1, requests), jnp.int32),
            pltpu.SMEM((members,), jnp.int32),
            pltpu.SMEM((members * PAIR,), jnp.int32),
            pltpu.SemaphoreType.DMA((3,)),
            pltpu.SemaphoreType.DMA,
        ],
        compiler_params=pltpu.CompilerParams(vmem_limit_bytes=32 * MIB),
        name="pack_pages",
    )(me, *(pltpu.with_memory_space_constraint(a, pltpu.HBM) for a in (dest, slot, length, pages)))


def sort_some(at, source, order, limit, keys, values_t):
    kv_heads, _, width = keys.shape
    kinds = 2 * kv_heads
    depth = 256 // kinds
    many = source.shape[0] // kinds
    parts = [source[256 * i : 256 * (i + 1), :] for i in range(many // depth)]
    done = nn_dot(order, jnp.concatenate(parts, axis=1))
    parts = [done[:, i * width : (i + 1) * width] for i in range(len(parts))]
    live = at + lax.broadcasted_iota(jnp.int32, (many, width), 0) < limit
    for kind in range(kinds):
        rows = jnp.concatenate([p[kind * depth : (kind + 1) * depth] for p in parts], axis=0)
        rows = jnp.where(live, rows, 0.0).astype(BF16)
        if kind < kv_heads:
            keys[kind, at : at + many, :] = rows
        else:
            values_t[kind - kv_heads, 0:width, at : at + many] = rows.T


def attend(scale, at, exact, context, prefix, q_ref, keys, values_t, mixed, staged, out_ref, sems):
    kv_heads, block, group, width = mixed.shape
    rows = block * group
    count = context + (at + 1) * block
    here = pl.ds(at * block, block)
    fine = jnp.ones((8, rows), F32)
    copies = []
    for h in range(kv_heads):
        q = q_ref[0, here, h * group : (h + 1) * group, :].astype(F32).reshape(rows, width)
        scores = nt_dot(twice(keys[h, :count]), scaled_queries(q, scale))
        key = lax.broadcasted_iota(jnp.int32, (block, rows), 0)
        row = lax.broadcasted_iota(jnp.int32, (block, rows), 1) // group
        if exact:
            dead = lax.broadcasted_iota(jnp.int32, (context, rows), 0) >= prefix
            first = jnp.where(dead, NEG, scores[:context])
            last = jnp.where(key <= row, scores[count - block :], NEG)
            middle = [scores[context : count - block]] if at else []
            scores = jnp.concatenate([first, *middle, last], axis=0)
            weights = jnp.exp2(scores - jnp.max(scores, axis=0, keepdims=True))
        else:
            weights = jnp.exp2(scores)
            last = jnp.where(key <= row, weights[count - block :], 0.0)
            weights = jnp.concatenate([weights[: count - block], last], axis=0)
        summed = nn_dot(values_t[h, :, :count], weights.astype(BF16))
        total_weight = summed[width : width + 8]
        fine = jnp.where(total_weight >= LOW, jnp.where(total_weight <= HIGH, fine, 0.0), 0.0)
        mixed[h] = (summed[:width] / total_weight[0:1]).T.reshape(block, group, width)
        if h % 2:
            some = pl.ds((h - 1) * group, 2 * group)
            staged[here, some, :] = jnp.concatenate([mixed[h - 1], mixed[h]], axis=1).astype(BF16)
            copies.append(
                pltpu.make_async_copy(
                    staged.at[here, some, :], out_ref.at[0, here, some, :], sems.at[at, h // 2]
                )
            )
            copies[-1].start()
    return fine, copies


def sort_kernel(scale, slots, prefix_ref, cached_hbm, q_hbm, cache_hbm, fresh_hbm, own_hbm, *refs):
    keys, values_t, scaled_ref, *state = refs[:6]
    some_keys, some_values, cached, step_q, cache, fresh, own, in_sems, sems = refs[6:]
    count = step_q.shape[0]
    kv_heads, total, width = keys.shape
    kinds = 2 * kv_heads
    context = cache.shape[0] // kinds
    tail_count = total - context
    prefix = prefix_ref[0]
    many = 128 * kinds
    loads = []
    for i in range(in_sems.shape[0]):
        size = cache.shape[0] // in_sems.shape[0]
        part = pl.ds(i * size, size)
        loads.append(pltpu.make_async_copy(cache_hbm.at[part, :], cache.at[part, :], in_sems.at[i]))
    others = [
        pltpu.make_async_copy(fresh_hbm, fresh, sems.at[0]),
        pltpu.make_async_copy(own_hbm, own, sems.at[1]),
        pltpu.make_async_copy(q_hbm.at[0, pl.ds(tail_count, count)], step_q, sems.at[2]),
    ]
    others.append(pltpu.make_async_copy(cached_hbm, cached, sems.at[3]))
    for copy in others + loads:
        copy.start()
    order = unmix(kinds, 256)
    extra = values_t.shape[1] - width
    lane = lax.broadcasted_iota(jnp.int32, (extra, total), 1)
    ones = jnp.where((lane < prefix) | (lane >= context), 1.0, 0.0).astype(BF16)
    for h in range(kv_heads):
        values_t[h, width:, :] = ones
    for copy in others:
        copy.wait()
    start_decode(
        scale, slots, cached, step_q, own, fresh, tail_count, scaled_ref, state, some_keys, some_values
    )
    for i in range(tail_count // 128):
        sort_some(
            context + i * 128, fresh.at[pl.ds(i * many, many), :], order, total, keys, values_t
        )
    per = context // 128 // len(loads)
    for i in range(context // 128):
        if i % per == 0:
            loads[i // per].wait()
        sort_some(i * 128, cache.at[pl.ds(i * many, many), :], order, prefix, keys, values_t)


def far_off(a):
    return pltpu.with_memory_space_constraint(a, pltpu.HBM)


def sort_keys(prefix, cached, queries, cache, fresh, own, tail_count, kv_heads):
    _, row_count, heads, width = queries.shape
    kinds = 2 * kv_heads
    context = cache.shape[0] // kinds
    total = context + tail_count
    count = row_count - tail_count
    rows = count * heads // kv_heads
    local = own.shape[0] // kinds + count
    scale = math.log2(math.e) / math.sqrt(width)
    smem = pl.BlockSpec(memory_space=pltpu.SMEM)
    vmem = pl.BlockSpec(memory_space=pltpu.VMEM)
    hbm = pl.BlockSpec(memory_space=pltpu.HBM)
    state = jax.ShapeDtypeStruct((kv_heads, rows, width), F32)
    return pl.pallas_call(
        functools.partial(sort_kernel, scale, cached.shape[1]),
        out_shape=[
            jax.ShapeDtypeStruct((kv_heads, total, width), BF16),
            jax.ShapeDtypeStruct((kv_heads, width + 16, total), BF16),
            jax.ShapeDtypeStruct((kv_heads, rows, 2 * width), BF16),
            state,
            state,
            state,
        ],
        in_specs=[smem, hbm, hbm, hbm, hbm, hbm],
        out_specs=[vmem] * 6,
        scratch_shapes=[
            pltpu.VMEM((kv_heads, local, width), BF16),
            pltpu.VMEM((kv_heads, local, width), BF16),
            pltpu.SMEM(cached.shape, jnp.int32),
            pltpu.VMEM((count, heads, width), BF16),
            pltpu.VMEM(cache.shape, BF16),
            pltpu.VMEM(fresh.shape, BF16),
            pltpu.VMEM(own.shape, BF16),
            pltpu.SemaphoreType.DMA((1,)),
            pltpu.SemaphoreType.DMA((4,)),
        ],
        compiler_params=pltpu.CompilerParams(vmem_limit_bytes=24 * MIB),
        cost_estimate=pl.CostEstimate(flops=1, bytes_accessed=12 * MIB, transcendentals=0),
        name="sort_keys",
    )(prefix, *(far_off(a) for a in (cached, queries, cache, fresh, own)))


def tail_kernel(scale, context, prefix_ref, q_ref, keys, values_t, out_ref, mixed, staged, sems):
    block = mixed.shape[1]
    prefix = prefix_ref[0]
    results = []
    for at in range(staged.shape[0] // block):
        results.append(
            attend(scale, at, False, context, prefix, q_ref, keys, values_t, mixed, staged, out_ref, sems)
        )
    for at, (fine, copies) in enumerate(results):
        for copy in copies:
            copy.wait()

        @pl.when(jnp.min(fine) < 0.5)
        def _():
            _, again = attend(
                scale, at, True, context, prefix, q_ref, keys, values_t, mixed, staged, out_ref, sems
            )
            for copy in again:
                copy.wait()


def tail_attention(prefix, queries, keys, values_t, tail_count):
    _, row_count, heads, width = queries.shape
    kv_heads, total, _ = keys.shape
    block = min(128, tail_count)
    group = heads // kv_heads
    scale = math.log2(math.e) / math.sqrt(width)
    smem = pl.BlockSpec(memory_space=pltpu.SMEM)
    vmem = pl.BlockSpec(memory_space=pltpu.VMEM)
    hbm = pl.BlockSpec(memory_space=pltpu.HBM)
    return pl.pallas_call(
        functools.partial(tail_kernel, scale, total - tail_count),
        out_shape=jax.ShapeDtypeStruct(queries.shape, BF16),
        in_specs=[smem] + [vmem] * 3,
        out_specs=hbm,
        scratch_shapes=[
            pltpu.VMEM((kv_heads, block, group, width), F32),
            pltpu.VMEM((tail_count, heads, width), BF16),
            pltpu.SemaphoreType.DMA((tail_count // block, kv_heads // 2)),
        ],
        compiler_params=pltpu.CompilerParams(vmem_limit_bytes=36 * MIB),
        cost_estimate=pl.CostEstimate(
            flops=16 * tail_count * heads * total * width,
            bytes_accessed=8 * MIB,
            transcendentals=tail_count * heads * total,
        ),
        name="tail_attention",
    )(prefix, queries, keys, values_t)


def row_place(rows, columns, group, slots):
    row = lax.broadcasted_iota(jnp.int32, (rows, columns), 0) // group
    return row % slots, row // slots


def split_rows(rows, base, keys, values):
    kv_heads = keys.shape[0]
    depth = rows.shape[0] // (2 * kv_heads)
    for h in range(kv_heads):
        keys[h, base : base + depth, :] = rows[h * depth : (h + 1) * depth]
        values[h, base : base + depth, :] = rows[(kv_heads + h) * depth : (kv_heads + h + 1) * depth]


def start_decode(scale, slots, cached_ref, q_ref, own_ref, fresh_ref, tail_count, scaled_ref, state, keys, values):
    count, heads, width = q_ref.shape
    kv_heads = keys.shape[0]
    group = heads // kv_heads
    kinds = 2 * kv_heads
    own_count = own_ref.shape[0] // kinds
    total = own_count + count
    chunk = min(256, own_ref.shape[0])
    order = unmix(kinds, chunk)
    for at in range(own_ref.shape[0] // chunk):
        rows = nn_dot(order, own_ref[at * chunk : (at + 1) * chunk, :]).astype(BF16)
        split_rows(rows, at * chunk // kinds, keys, values)
    chunk = min(256, count * kinds)
    order = unmix(kinds, chunk)
    for at in range(count * kinds // chunk):
        begin = tail_count * kinds + at * chunk
        rows = nn_dot(order, fresh_ref[begin : begin + chunk, :]).astype(BF16)
        split_rows(rows, own_count + at * chunk // kinds, keys, values)
    rows = count * group
    key = lax.broadcasted_iota(jnp.int32, (1, total), 1)
    depth = own_count // slots
    code = jnp.where(key < own_count, -1, (key - own_count) % slots)
    for s in range(slots):
        mine = jnp.where(key < own_count, key // depth, -1) == s
        code = jnp.where(mine & (key % depth < cached_ref[0, s]), s, code)
    since = jnp.where(key < own_count, 0, (key - own_count) // slots)
    slot, made = row_place(rows, total, group, slots)
    allowed = (code == slot) & (since <= made)
    queries = q_ref[...].astype(F32).reshape(count, kv_heads, group, width)
    peaks, sums, mixes = state
    for h in range(kv_heads):
        q = scaled_queries(queries[:, h].reshape(rows, width), scale)
        scaled_ref[h] = q
        scores = jnp.where(allowed, nt_dot(q, twice(keys[h, :total])), NEG)
        peak = jnp.max(scores, axis=1, keepdims=True)
        weights = jnp.exp2(scores - peak).astype(BF16)
        summed = nn_dot(weights, with_ones(values[h, :total]))
        peaks[h] = jnp.broadcast_to(peak, (rows, width))
        sums[h] = summed[:, width:]
        mixes[h] = summed[:, :width]


def add_pages(slots, group, buffers, scaled_ref, state, finish, keys, values):
    kv_heads, rows, width = state[0].shape
    kinds = 2 * kv_heads
    page_rows = (buffers[0].shape[0] - META) // PAIR
    depth = page_rows // kinds
    order = unmix(kinds, page_rows)
    lane = lax.broadcasted_iota(jnp.int32, (1, 128), 1)
    codes = []
    for k, buffer in enumerate(buffers):
        both = [buffer[half * page_rows : (half + 1) * page_rows, :] for half in range(PAIR)]
        done = nn_dot(order, jnp.concatenate(both, axis=1)).astype(BF16)
        for half in range(PAIR):
            split_rows(
                done[:, half * width : (half + 1) * width], (PAIR * k + half) * depth, keys, values
            )
        codes.append(buffer[PAIR * page_rows : PAIR * page_rows + META, :].astype(F32)[0:1, :])
    code = jnp.concatenate(
        [jnp.where(lane < 64, codes[k], codes[k + 1]) for k in range(0, len(codes), 2)], axis=1
    )
    total = code.shape[1]
    slot, _ = row_place(rows, total, group, slots)
    allowed = code == slot.astype(F32)
    peaks, sums, mixes = state
    for h in range(kv_heads):
        old_peak = peaks[h]
        scores = jnp.where(allowed, nt_dot(scaled_ref[h], twice(keys[h, :total])), NEG)
        peak = jnp.maximum(old_peak, jnp.max(scores, axis=1, keepdims=True))
        weights = jnp.exp2(scores - peak[:, 0:1]).astype(BF16)
        summed = nn_dot(weights, with_ones(values[h, :total]))
        shrink = jnp.exp2(old_peak - peak)
        weight_sum = sums[h] * shrink + summed[:, width:]
        mix = mixes[h] * shrink + summed[:, :width]
        if finish:
            finish(h, weight_sum, mix)
        else:
            for kept, new in zip(state, (peak, weight_sum, mix)):
                kept[h] = new


def page_kernel(slots, scaled_ref, m_in, l_in, a_in, out_in, *refs):
    *arrived, out_ref, peaks, sums, mixes, keys, values, mixed, staged, sems = refs
    kv_heads, count, group, width = mixed.shape
    given, state = (m_in, l_in, a_in), (peaks, sums, mixes)
    tail_count = out_ref.shape[1] - count
    copies = []

    def finish(h, weight_sum, mix):
        mixed[h] = (mix / weight_sum).reshape(count, group, width)
        if h % 2:
            some = pl.ds((h - 1) * group, 2 * group)
            staged[:, some, :] = jnp.concatenate([mixed[h - 1], mixed[h]], axis=1).astype(BF16)
            copies.append(
                pltpu.make_async_copy(
                    staged.at[:, some, :],
                    out_ref.at[0, pl.ds(tail_count, count), some, :],
                    sems.at[h // 2],
                )
            )
            copies[-1].start()

    if len(arrived) > 1:
        add_pages(slots, group, arrived, scaled_ref, given, finish, keys, values)
    else:
        buffers = arrived[0]
        per = keys.shape[1] // 64
        for kept, old in zip(state, given):
            kept[...] = old[...]

        def some_pages(i, _):
            part = [buffers.at[i * per + k] for k in range(per)]
            add_pages(slots, group, part, scaled_ref, state, None, keys, values)
            return 0

        lax.fori_loop(0, buffers.shape[0] // per, some_pages, 0)
        for h in range(kv_heads):
            finish(h, sums[h], mixes[h])
    for copy in copies:
        copy.wait()


def page_attention(scaled, state, out, arrived, slots):
    kv_heads, rows, width = state[0].shape
    heads = out.shape[2]
    group = heads // kv_heads
    count = rows // group
    chunk = 64 * (len(arrived) if len(arrived) > 1 else 8)
    vmem = pl.BlockSpec(memory_space=pltpu.VMEM)
    hbm = pl.BlockSpec(memory_space=pltpu.HBM)
    return pl.pallas_call(
        functools.partial(page_kernel, slots),
        out_shape=jax.ShapeDtypeStruct(out.shape, BF16),
        in_specs=[vmem] * 4 + [hbm] + [vmem] * len(arrived),
        out_specs=hbm,
        input_output_aliases={4: 0},
        scratch_shapes=[pltpu.VMEM(state[0].shape, F32)] * 3
        + [
            pltpu.VMEM((kv_heads, chunk, width), BF16),
            pltpu.VMEM((kv_heads, chunk, width), BF16),
            pltpu.VMEM((kv_heads, count, group, width), F32),
            pltpu.VMEM((count, heads, width), BF16),
            pltpu.SemaphoreType.DMA((kv_heads // 2,)),
        ],
        compiler_params=pltpu.CompilerParams(vmem_limit_bytes=48 * MIB),
        name="decode_pages",
    )(scaled, *state, out, *arrived)


def body(
    request_dest,
    request_slot,
    page_len,
    page_rows,
    kv_cache,
    decode_cache,
    prefix_len,
    cached_len,
    queries,
    fresh_kv,
):
    members = lax.axis_size("inst")
    slots = cached_len.shape[1]
    row_count, heads, width = queries.shape[1:]
    kv_heads = kv_cache.shape[3]
    tail_count = row_count - 2 * slots
    requests, page_depth = page_rows.shape[1:3]
    split = members <= 8
    me = lax.axis_index("inst").astype(jnp.int32)

    pages = page_rows.reshape(requests, page_depth * 2 * kv_heads, width)
    packed = pack(split, members, me.reshape(1), request_dest, request_slot, page_len, pages)
    keys, values_t, scaled, *state = sort_keys(
        prefix_len,
        cached_len,
        queries,
        kv_cache.reshape(-1, width),
        fresh_kv.reshape(-1, width),
        decode_cache.reshape(-1, width),
        tail_count,
        kv_heads,
    )
    if split:
        half = members // 2
        far = [half + i for i in FAR_ORDER] if half == len(FAR_ORDER) else list(range(half, members))
        swap = lambda block, k: lax.ppermute(block, "inst", [(i, i ^ k) for i in range(members)])
        arrived = list(packed)
        for k in [*far[: half - 2], *range(1, half)]:
            arrived[k] = swap(packed[k], k)
        later = far[half - 2 :]
        keys, arrived[far[0]], *blocks = lax.optimization_barrier(
            (keys, arrived[far[0]], *(packed[k] for k in later))
        )
        for k, block in zip(later, blocks):
            arrived[k] = swap(block, k)
    else:
        arrived = [lax.all_to_all(packed[0], "inst", split_axis=0, concat_axis=0, tiled=True)]
    out = tail_attention(prefix_len, queries, keys, values_t, tail_count)
    if split:
        arrived = arrived[:half] + [arrived[k] for k in far]
    return page_attention(scaled, state, out, arrived, slots)


def solution(mesh):
    placed = (
        P(("groups", "inst"), None),
        P(("groups", "inst"), None),
        P(("groups", "inst"), None),
        P(("groups", "inst"), None, None, None, "tp", None),
        P(("groups", "inst"), None, None, "tp", None),
        P(("groups", "inst"), None, None, "tp", None),
        P(("groups", "inst")),
        P(("groups", "inst"), None),
        P(("groups", "inst"), None, "tp", None),
        P(("groups", "inst"), None, None, "tp", None),
    )
    return jax.shard_map(
        body,
        mesh=mesh,
        in_specs=placed,
        out_specs=P(("groups", "inst"), None, "tp", None),
        check_vma=False,
    )
```

```python
import functools
import math

import jax
import jax.numpy as jnp
from jax import lax
from jax.experimental import pallas as pl
from jax.experimental.pallas import tpu as pltpu
from jax.sharding import PartitionSpec as P

PAIR = 2
NEG = -1e30
F32 = jnp.float32
BF16 = jnp.bfloat16
META = 8
MIB = 1 << 20
FAR_ORDER = (0, 3, 1, 2)
LOW, HIGH = 2.0**-40, 2.0**120


def nt_dot(a, b):
    return lax.dot_general(a, b, (((1,), (1,)), ((), ())), preferred_element_type=F32)


def nn_dot(a, b):
    return jnp.dot(a, b, preferred_element_type=F32)


def unmix(kinds, rows):
    keys = rows // kinds
    i = lax.broadcasted_iota(jnp.int32, (rows, rows), 0)
    j = lax.broadcasted_iota(jnp.int32, (rows, rows), 1)
    return jnp.where(j == (i % keys) * kinds + i // keys, 1.0, 0.0).astype(BF16)


def scaled_queries(q, scale):
    q = q * scale
    high = q.astype(BF16)
    low = (q - high.astype(F32)).astype(BF16)
    return jnp.concatenate([high, low], axis=1)


def twice(k):
    return jnp.concatenate([k, k], axis=1)


def with_ones(v):
    return jnp.concatenate([v, jnp.ones_like(v)], axis=1)


def pack_kernel(split, me_ref, dest_hbm, slot_hbm, len_hbm, pages_hbm, *refs):
    *buffers, pages, dest, slot, length, count, table, small_sem, page_sem = refs
    requests, page_rows = pages.shape[:2]
    members = len(buffers) if split else buffers[0].shape[0]
    small = [
        pltpu.make_async_copy(source, target, small_sem.at[i])
        for i, (source, target) in enumerate(
            ((dest_hbm, dest), (slot_hbm, slot), (len_hbm, length))
        )
    ]
    large = pltpu.make_async_copy(pages_hbm, pages, page_sem)
    for copy in small:
        copy.start()
    large.start()

    def clear(k, _):
        count[k] = 0
        for half in range(PAIR):
            table[k * PAIR + half] = -1
        return 0

    lax.fori_loop(0, members, clear, 0)
    for copy in small:
        copy.wait()
    me = me_ref[0]

    def place(r, _):
        peer = dest[0, r] ^ me if split else dest[0, r]
        at = count[peer]
        count[peer] = at + 1
        table[peer * PAIR + at] = r
        return 0

    lax.fori_loop(0, requests, place, 0)
    lane = lax.broadcasted_iota(jnp.int32, (META, 128), 1)
    depth = 128 // (2 * PAIR)
    half_of, key_of = (lane // depth) % PAIR, lane % depth

    def fill(k, buffer):
        code = jnp.full((META, 128), -1.0, F32)
        for half in range(PAIR):
            r = table[k * PAIR + half]
            known = jnp.maximum(r, 0)
            live = jnp.where(r >= 0, length[0, known], 0)
            here = jnp.where(half_of == half, key_of, depth) < live
            code = jnp.where(here, slot[0, known].astype(F32), code)
            buffer[half * page_rows : (half + 1) * page_rows, :] = jnp.where(
                r >= 0, pages[known], jnp.zeros((page_rows, 128), BF16)
            )
        buffer[PAIR * page_rows : PAIR * page_rows + META, :] = code.astype(BF16)

    large.wait()
    if split:
        for k in range(members):
            fill(k, buffers[k])
    else:

        def fill_one(k, _):
            fill(k, buffers[0].at[k])
            return 0

        lax.fori_loop(0, members, fill_one, 0)


def pack(split, members, me, dest, slot, length, pages):
    requests, page_rows = pages.shape[:2]
    rows = PAIR * page_rows + META
    if split:
        out_shape = [jax.ShapeDtypeStruct((rows, 128), BF16)] * members
    else:
        out_shape = [jax.ShapeDtypeStruct((members, rows, 128), BF16)]
    return pl.pallas_call(
        functools.partial(pack_kernel, split),
        out_shape=out_shape,
        in_specs=[pl.BlockSpec(memory_space=pltpu.SMEM)] + [pl.BlockSpec(memory_space=pltpu.HBM)] * 4,
        out_specs=[pl.BlockSpec(memory_space=pltpu.VMEM)] * len(out_shape),
        scratch_shapes=[
            pltpu.VMEM(pages.shape, BF16),
            pltpu.SMEM((1, requests), jnp.int32),
            pltpu.SMEM((1, requests), jnp.int32),
            pltpu.SMEM((1, requests), jnp.int32),
            pltpu.SMEM((members,), jnp.int32),
            pltpu.SMEM((members * PAIR,), jnp.int32),
            pltpu.SemaphoreType.DMA((3,)),
            pltpu.SemaphoreType.DMA,
        ],
        compiler_params=pltpu.CompilerParams(vmem_limit_bytes=32 * MIB),
        name="pack_pages",
    )(me, *(pltpu.with_memory_space_constraint(a, pltpu.HBM) for a in (dest, slot, length, pages)))


def sort_some(at, source, order, limit, keys, values_t):
    kv_heads, _, width = keys.shape
    kinds = 2 * kv_heads
    depth = 256 // kinds
    many = source.shape[0] // kinds
    parts = [source[256 * i : 256 * (i + 1), :] for i in range(many // depth)]
    done = nn_dot(order, jnp.concatenate(parts, axis=1))
    parts = [done[:, i * width : (i + 1) * width] for i in range(len(parts))]
    live = at + lax.broadcasted_iota(jnp.int32, (many, width), 0) < limit
    for kind in range(kinds):
        rows = jnp.concatenate([p[kind * depth : (kind + 1) * depth] for p in parts], axis=0)
        rows = jnp.where(live, rows, 0.0).astype(BF16)
        if kind < kv_heads:
            keys[kind, at : at + many, :] = rows
        else:
            values_t[kind - kv_heads, 0:width, at : at + many] = rows.T


def attend(scale, at, exact, context, prefix, q_ref, keys, values_t, mixed, staged, out_ref, sems):
    kv_heads, block, group, width = mixed.shape
    rows = block * group
    count = context + (at + 1) * block
    here = pl.ds(at * block, block)
    fine = jnp.ones((8, rows), F32)
    copies = []
    for h in range(kv_heads):
        q = q_ref[0, here, h * group : (h + 1) * group, :].astype(F32).reshape(rows, width)
        scores = nt_dot(twice(keys[h, :count]), scaled_queries(q, scale))
        key = lax.broadcasted_iota(jnp.int32, (block, rows), 0)
        row = lax.broadcasted_iota(jnp.int32, (block, rows), 1) // group
        if exact:
            dead = lax.broadcasted_iota(jnp.int32, (context, rows), 0) >= prefix
            first = jnp.where(dead, NEG, scores[:context])
            last = jnp.where(key <= row, scores[count - block :], NEG)
            middle = [scores[context : count - block]] if at else []
            scores = jnp.concatenate([first, *middle, last], axis=0)
            weights = jnp.exp2(scores - jnp.max(scores, axis=0, keepdims=True))
        else:
            weights = jnp.exp2(scores)
            last = jnp.where(key <= row, weights[count - block :], 0.0)
            weights = jnp.concatenate([weights[: count - block], last], axis=0)
        summed = nn_dot(values_t[h, :, :count], weights.astype(BF16))
        total_weight = summed[width : width + 8]
        fine = jnp.where(total_weight >= LOW, jnp.where(total_weight <= HIGH, fine, 0.0), 0.0)
        mixed[h] = (summed[:width] / total_weight[0:1]).T.reshape(block, group, width)
        if h % 2:
            some = pl.ds((h - 1) * group, 2 * group)
            staged[here, some, :] = jnp.concatenate([mixed[h - 1], mixed[h]], axis=1).astype(BF16)
            copies.append(
                pltpu.make_async_copy(
                    staged.at[here, some, :], out_ref.at[0, here, some, :], sems.at[at, h // 2]
                )
            )
            copies[-1].start()
    return fine, copies


def sort_kernel(scale, slots, prefix_ref, cached_hbm, q_hbm, cache_hbm, fresh_hbm, own_hbm, *refs):
    keys, values_t, scaled_ref, *state = refs[:6]
    some_keys, some_values, cached, step_q, cache, fresh, own, in_sems, sems = refs[6:]
    count = step_q.shape[0]
    kv_heads, total, width = keys.shape
    kinds = 2 * kv_heads
    context = cache.shape[0] // kinds
    tail_count = total - context
    prefix = prefix_ref[0]
    many = 128 * kinds
    loads = []
    for i in range(in_sems.shape[0]):
        size = cache.shape[0] // in_sems.shape[0]
        part = pl.ds(i * size, size)
        loads.append(pltpu.make_async_copy(cache_hbm.at[part, :], cache.at[part, :], in_sems.at[i]))
    others = [
        pltpu.make_async_copy(fresh_hbm, fresh, sems.at[0]),
        pltpu.make_async_copy(own_hbm, own, sems.at[1]),
        pltpu.make_async_copy(q_hbm.at[0, pl.ds(tail_count, count)], step_q, sems.at[2]),
    ]
    others.append(pltpu.make_async_copy(cached_hbm, cached, sems.at[3]))
    for copy in others + loads:
        copy.start()
    order = unmix(kinds, 256)
    extra = values_t.shape[1] - width
    lane = lax.broadcasted_iota(jnp.int32, (extra, total), 1)
    ones = jnp.where((lane < prefix) | (lane >= context), 1.0, 0.0).astype(BF16)
    for h in range(kv_heads):
        values_t[h, width:, :] = ones
    for copy in others:
        copy.wait()
    start_decode(
        scale, slots, cached, step_q, own, fresh, tail_count, scaled_ref, state, some_keys, some_values
    )
    for i in range(tail_count // 128):
        sort_some(
            context + i * 128, fresh.at[pl.ds(i * many, many), :], order, total, keys, values_t
        )
    per = context // 128 // len(loads)
    for i in range(context // 128):
        if i % per == 0:
            loads[i // per].wait()
        sort_some(i * 128, cache.at[pl.ds(i * many, many), :], order, prefix, keys, values_t)


def far_off(a):
    return pltpu.with_memory_space_constraint(a, pltpu.HBM)


def sort_keys(prefix, cached, queries, cache, fresh, own, tail_count, kv_heads):
    _, row_count, heads, width = queries.shape
    kinds = 2 * kv_heads
    context = cache.shape[0] // kinds
    total = context + tail_count
    count = row_count - tail_count
    rows = count * heads // kv_heads
    local = own.shape[0] // kinds + count
    scale = math.log2(math.e) / math.sqrt(width)
    smem = pl.BlockSpec(memory_space=pltpu.SMEM)
    vmem = pl.BlockSpec(memory_space=pltpu.VMEM)
    hbm = pl.BlockSpec(memory_space=pltpu.HBM)
    state = jax.ShapeDtypeStruct((kv_heads, rows, width), F32)
    return pl.pallas_call(
        functools.partial(sort_kernel, scale, cached.shape[1]),
        out_shape=[
            jax.ShapeDtypeStruct((kv_heads, total, width), BF16),
            jax.ShapeDtypeStruct((kv_heads, width + 16, total), BF16),
            jax.ShapeDtypeStruct((kv_heads, rows, 2 * width), BF16),
            state,
            state,
            state,
        ],
        in_specs=[smem, hbm, hbm, hbm, hbm, hbm],
        out_specs=[vmem] * 6,
        scratch_shapes=[
            pltpu.VMEM((kv_heads, local, width), BF16),
            pltpu.VMEM((kv_heads, local, width), BF16),
            pltpu.SMEM(cached.shape, jnp.int32),
            pltpu.VMEM((count, heads, width), BF16),
            pltpu.VMEM(cache.shape, BF16),
            pltpu.VMEM(fresh.shape, BF16),
            pltpu.VMEM(own.shape, BF16),
            pltpu.SemaphoreType.DMA((1,)),
            pltpu.SemaphoreType.DMA((4,)),
        ],
        compiler_params=pltpu.CompilerParams(vmem_limit_bytes=24 * MIB),
        cost_estimate=pl.CostEstimate(flops=1, bytes_accessed=12 * MIB, transcendentals=0),
        name="sort_keys",
    )(prefix, *(far_off(a) for a in (cached, queries, cache, fresh, own)))


def tail_kernel(scale, context, prefix_ref, q_ref, keys, values_t, out_ref, mixed, staged, sems):
    block = mixed.shape[1]
    prefix = prefix_ref[0]
    results = []
    for at in range(staged.shape[0] // block):
        results.append(
            attend(scale, at, False, context, prefix, q_ref, keys, values_t, mixed, staged, out_ref, sems)
        )
    for at, (fine, copies) in enumerate(results):
        for copy in copies:
            copy.wait()

        @pl.when(jnp.min(fine) < 0.5)
        def _():
            _, again = attend(
                scale, at, True, context, prefix, q_ref, keys, values_t, mixed, staged, out_ref, sems
            )
            for copy in again:
                copy.wait()


def tail_attention(prefix, queries, keys, values_t, tail_count):
    _, row_count, heads, width = queries.shape
    kv_heads, total, _ = keys.shape
    block = min(128, tail_count)
    group = heads // kv_heads
    scale = math.log2(math.e) / math.sqrt(width)
    smem = pl.BlockSpec(memory_space=pltpu.SMEM)
    vmem = pl.BlockSpec(memory_space=pltpu.VMEM)
    hbm = pl.BlockSpec(memory_space=pltpu.HBM)
    return pl.pallas_call(
        functools.partial(tail_kernel, scale, total - tail_count),
        out_shape=jax.ShapeDtypeStruct(queries.shape, BF16),
        in_specs=[smem] + [vmem] * 3,
        out_specs=hbm,
        scratch_shapes=[
            pltpu.VMEM((kv_heads, block, group, width), F32),
            pltpu.VMEM((tail_count, heads, width), BF16),
            pltpu.SemaphoreType.DMA((tail_count // block, kv_heads // 2)),
        ],
        compiler_params=pltpu.CompilerParams(vmem_limit_bytes=36 * MIB),
        cost_estimate=pl.CostEstimate(
            flops=16 * tail_count * heads * total * width,
            bytes_accessed=8 * MIB,
            transcendentals=tail_count * heads * total,
        ),
        name="tail_attention",
    )(prefix, queries, keys, values_t)


def row_place(rows, columns, group, slots):
    row = lax.broadcasted_iota(jnp.int32, (rows, columns), 0) // group
    return row % slots, row // slots


def split_rows(rows, base, keys, values):
    kv_heads = keys.shape[0]
    depth = rows.shape[0] // (2 * kv_heads)
    for h in range(kv_heads):
        keys[h, base : base + depth, :] = rows[h * depth : (h + 1) * depth]
        values[h, base : base + depth, :] = rows[(kv_heads + h) * depth : (kv_heads + h + 1) * depth]


def start_decode(scale, slots, cached_ref, q_ref, own_ref, fresh_ref, tail_count, scaled_ref, state, keys, values):
    count, heads, width = q_ref.shape
    kv_heads = keys.shape[0]
    group = heads // kv_heads
    kinds = 2 * kv_heads
    own_count = own_ref.shape[0] // kinds
    total = own_count + count
    chunk = min(256, own_ref.shape[0])
    order = unmix(kinds, chunk)
    for at in range(own_ref.shape[0] // chunk):
        rows = nn_dot(order, own_ref[at * chunk : (at + 1) * chunk, :]).astype(BF16)
        split_rows(rows, at * chunk // kinds, keys, values)
    chunk = min(256, count * kinds)
    order = unmix(kinds, chunk)
    for at in range(count * kinds // chunk):
        begin = tail_count * kinds + at * chunk
        rows = nn_dot(order, fresh_ref[begin : begin + chunk, :]).astype(BF16)
        split_rows(rows, own_count + at * chunk // kinds, keys, values)
    rows = count * group
    key = lax.broadcasted_iota(jnp.int32, (1, total), 1)
    depth = own_count // slots
    code = jnp.where(key < own_count, -1, (key - own_count) % slots)
    for s in range(slots):
        mine = jnp.where(key < own_count, key // depth, -1) == s
        code = jnp.where(mine & (key % depth < cached_ref[0, s]), s, code)
    since = jnp.where(key < own_count, 0, (key - own_count) // slots)
    slot, made = row_place(rows, total, group, slots)
    allowed = (code == slot) & (since <= made)
    queries = q_ref[...].astype(F32).reshape(count, kv_heads, group, width)
    peaks, sums, mixes = state
    for h in range(kv_heads):
        q = scaled_queries(queries[:, h].reshape(rows, width), scale)
        scaled_ref[h] = q
        scores = jnp.where(allowed, nt_dot(q, twice(keys[h, :total])), NEG)
        peak = jnp.max(scores, axis=1, keepdims=True)
        weights = jnp.exp2(scores - peak).astype(BF16)
        summed = nn_dot(weights, with_ones(values[h, :total]))
        peaks[h] = jnp.broadcast_to(peak, (rows, width))
        sums[h] = summed[:, width:]
        mixes[h] = summed[:, :width]


def add_pages(slots, group, buffers, scaled_ref, state, finish, keys, values):
    kv_heads, rows, width = state[0].shape
    kinds = 2 * kv_heads
    page_rows = (buffers[0].shape[0] - META) // PAIR
    depth = page_rows // kinds
    order = unmix(kinds, page_rows)
    lane = lax.broadcasted_iota(jnp.int32, (1, 128), 1)
    codes = []
    for k, buffer in enumerate(buffers):
        both = [buffer[half * page_rows : (half + 1) * page_rows, :] for half in range(PAIR)]
        done = nn_dot(order, jnp.concatenate(both, axis=1)).astype(BF16)
        for half in range(PAIR):
            split_rows(
                done[:, half * width : (half + 1) * width], (PAIR * k + half) * depth, keys, values
            )
        codes.append(buffer[PAIR * page_rows : PAIR * page_rows + META, :].astype(F32)[0:1, :])
    code = jnp.concatenate(
        [jnp.where(lane < 64, codes[k], codes[k + 1]) for k in range(0, len(codes), 2)], axis=1
    )
    total = code.shape[1]
    slot, _ = row_place(rows, total, group, slots)
    allowed = code == slot.astype(F32)
    peaks, sums, mixes = state
    for h in range(kv_heads):
        old_peak = peaks[h]
        scores = jnp.where(allowed, nt_dot(scaled_ref[h], twice(keys[h, :total])), NEG)
        peak = jnp.maximum(old_peak, jnp.max(scores, axis=1, keepdims=True))
        weights = jnp.exp2(scores - peak[:, 0:1]).astype(BF16)
        summed = nn_dot(weights, with_ones(values[h, :total]))
        shrink = jnp.exp2(old_peak - peak)
        weight_sum = sums[h] * shrink + summed[:, width:]
        mix = mixes[h] * shrink + summed[:, :width]
        if finish:
            finish(h, weight_sum, mix)
        else:
            for kept, new in zip(state, (peak, weight_sum, mix)):
                kept[h] = new


def page_kernel(slots, scaled_ref, m_in, l_in, a_in, out_in, *refs):
    *arrived, out_ref, peaks, sums, mixes, keys, values, mixed, staged, sems = refs
    kv_heads, count, group, width = mixed.shape
    given, state = (m_in, l_in, a_in), (peaks, sums, mixes)
    tail_count = out_ref.shape[1] - count
    copies = []

    def finish(h, weight_sum, mix):
        mixed[h] = (mix / weight_sum).reshape(count, group, width)
        if h % 2:
            some = pl.ds((h - 1) * group, 2 * group)
            staged[:, some, :] = jnp.concatenate([mixed[h - 1], mixed[h]], axis=1).astype(BF16)
            copies.append(
                pltpu.make_async_copy(
                    staged.at[:, some, :],
                    out_ref.at[0, pl.ds(tail_count, count), some, :],
                    sems.at[h // 2],
                )
            )
            copies[-1].start()

    if len(arrived) > 1:
        add_pages(slots, group, arrived, scaled_ref, given, finish, keys, values)
    else:
        buffers = arrived[0]
        per = keys.shape[1] // 64
        for kept, old in zip(state, given):
            kept[...] = old[...]

        def some_pages(i, _):
            part = [buffers.at[i * per + k] for k in range(per)]
            add_pages(slots, group, part, scaled_ref, state, None, keys, values)
            return 0

        lax.fori_loop(0, buffers.shape[0] // per, some_pages, 0)
        for h in range(kv_heads):
            finish(h, sums[h], mixes[h])
    for copy in copies:
        copy.wait()


def page_attention(scaled, state, out, arrived, slots):
    kv_heads, rows, width = state[0].shape
    heads = out.shape[2]
    group = heads // kv_heads
    count = rows // group
    chunk = 64 * (len(arrived) if len(arrived) > 1 else 8)
    vmem = pl.BlockSpec(memory_space=pltpu.VMEM)
    hbm = pl.BlockSpec(memory_space=pltpu.HBM)
    return pl.pallas_call(
        functools.partial(page_kernel, slots),
        out_shape=jax.ShapeDtypeStruct(out.shape, BF16),
        in_specs=[vmem] * 4 + [hbm] + [vmem] * len(arrived),
        out_specs=hbm,
        input_output_aliases={4: 0},
        scratch_shapes=[pltpu.VMEM(state[0].shape, F32)] * 3
        + [
            pltpu.VMEM((kv_heads, chunk, width), BF16),
            pltpu.VMEM((kv_heads, chunk, width), BF16),
            pltpu.VMEM((kv_heads, count, group, width), F32),
            pltpu.VMEM((count, heads, width), BF16),
            pltpu.SemaphoreType.DMA((kv_heads // 2,)),
        ],
        compiler_params=pltpu.CompilerParams(vmem_limit_bytes=48 * MIB),
        name="decode_pages",
    )(scaled, *state, out, *arrived)


def body(
    request_dest,
    request_slot,
    page_len,
    page_rows,
    kv_cache,
    decode_cache,
    prefix_len,
    cached_len,
    queries,
    fresh_kv,
):
    members = lax.axis_size("inst")
    slots = cached_len.shape[1]
    row_count, heads, width = queries.shape[1:]
    kv_heads = kv_cache.shape[3]
    tail_count = row_count - 2 * slots
    requests, page_depth = page_rows.shape[1:3]
    split = members <= 8
    me = lax.axis_index("inst").astype(jnp.int32)

    pages = page_rows.reshape(requests, page_depth * 2 * kv_heads, width)
    packed = pack(split, members, me.reshape(1), request_dest, request_slot, page_len, pages)
    keys, values_t, scaled, *state = sort_keys(
        prefix_len,
        cached_len,
        queries,
        kv_cache.reshape(-1, width),
        fresh_kv.reshape(-1, width),
        decode_cache.reshape(-1, width),
        tail_count,
        kv_heads,
    )
    if split:
        half = members // 2
        far = [half + i for i in FAR_ORDER] if half == len(FAR_ORDER) else list(range(half, members))
        swap = lambda block, k: lax.ppermute(block, "inst", [(i, i ^ k) for i in range(members)])
        arrived = list(packed)
        for k in [*far[: half - 2], *range(1, half)]:
            arrived[k] = swap(packed[k], k)
        later = far[half - 2 :]
        keys, arrived[far[0]], *blocks = lax.optimization_barrier(
            (keys, arrived[far[0]], *(packed[k] for k in later))
        )
        for k, block in zip(later, blocks):
            arrived[k] = swap(block, k)
    else:
        arrived = [lax.all_to_all(packed[0], "inst", split_axis=0, concat_axis=0, tiled=True)]
    out = tail_attention(prefix_len, queries, keys, values_t, tail_count)
    if split:
        arrived = arrived[:half] + [arrived[k] for k in far]
    return page_attention(scaled, state, out, arrived, slots)


def solution(mesh):
    placed = (
        P(("groups", "inst"), None),
        P(("groups", "inst"), None),
        P(("groups", "inst"), None),
        P(("groups", "inst"), None, None, None, "tp", None),
        P(("groups", "inst"), None, None, "tp", None),
        P(("groups", "inst"), None, None, "tp", None),
        P(("groups", "inst")),
        P(("groups", "inst"), None),
        P(("groups", "inst"), None, "tp", None),
        P(("groups", "inst"), None, None, "tp", None),
    )
    return jax.shard_map(
        body,
        mesh=mesh,
        in_specs=placed,
        out_specs=P(("groups", "inst"), None, "tp", None),
        check_vma=False,
    )
```
